256 devices in a mesh: stretch: 4 (over z_hi), space: 64 (over x, y, z_lo, core).
Axes of the slice: x: 4, y: 4, z: 8 (z_hi: 4, z_lo: 2; z = z_hi * 2 + z_lo), core: 2. Of those that a mesh axis runs over, the one named last changes fastest.
Arguments:
- queries: bfloat16 [4, 1024, 3072], P('stretch', 'space'), may hold values from -8 to 8
- stretch_keys: bfloat16 [4, 1024, 3072], P('stretch', 'space'), may hold values from -4 to 4
- stretch_values: bfloat16 [4, 1024, 3072], P('stretch', 'space'), may hold values from -6 to 6
- cache_keys: bfloat16 [32, 1024, 3072], P('stretch', 'space'), may hold values from -4 to 4
- cache_values: bfloat16 [32, 1024, 3072], P('stretch', 'space'), may hold values from -6 to 6
- block_list: int32 [4, 16], replicated, may hold values from 0 to 31, as said below
- list_len: int32 [4], replicated, may hold values from 4 to 16
- tok_count: int32 [4], replicated, may hold values from 512 to 1024, as said below
- noise_levels: int32 [4], replicated, may hold values from 0 to 47
- gate_table: float32 [48, 3072], replicated, may hold values from 0.1 to 1.9
Outputs:
- shifted: bfloat16 [4, 1024, 3072], P('stretch', 'space')
The draws below stay inside these ranges and needn't reach their ends.
Inputs may be any that keep to these rules, and one draw needn't show every extreme that they name: `block_list`: stretch c's list names list_len[c] distinct blocks; the owner of block b is b // 8; at most 4 of one list's blocks have one owner, and every list has exactly 4 from some owner; in every draw one stretch's list is full, with 4 blocks from every owner, and another stretch's list holds exactly 4 blocks; entries from list_len[c] on are 0. `tok_count`: some stretch has all 1024 slots valid in every draw.
All inputs are finite; a program needn't handle non-finite values.
Results may differ from the reference program's by a relative error of at most 0.025.
Values may be sent and summed in bfloat16 or wider, within the bound.
A program may use at most 128 MiB of HBM per device.

```python
import math
import jax
import jax.numpy as jnp
from jax import lax

HEADS = 24
HEAD_DIM = 128
G_DEV = 8
PER_SRC = 4
LEVELS = 48
FEATURES = 3072
STRETCHES = 4
STRETCH_TOK = 1024
BLOCKS = 32
LIST = 16


def list_parts(key):
    key = jax.random.fold_in(key, 11)
    counts = jax.random.randint(jax.random.fold_in(key, 1), (STRETCHES, STRETCHES), 0, PER_SRC + 1)
    full_owner = jax.random.randint(jax.random.fold_in(key, 2), (STRETCHES,), 0, STRETCHES)
    owner_ids = jnp.arange(STRETCHES)
    counts = jnp.where(owner_ids[None, :] == full_owner[:, None], PER_SRC, counts)
    full_stretch = jax.random.randint(jax.random.fold_in(key, 4), (), 0, STRETCHES)
    sparse_stretch = (full_stretch + 1 + jax.random.randint(jax.random.fold_in(key, 7), (), 0, STRETCHES - 1)) % STRETCHES
    counts = jnp.where((owner_ids == full_stretch)[:, None], PER_SRC, counts)
    sparse_row = jnp.where(owner_ids == full_owner[sparse_stretch], PER_SRC, 0)
    counts = jnp.where((owner_ids == sparse_stretch)[:, None], sparse_row[None, :], counts)
    shuffled = jax.vmap(lambda sub: jax.random.permutation(sub, G_DEV))(jax.random.split(jax.random.fold_in(key, 3), STRETCHES * STRETCHES))
    shuffled = shuffled.reshape(STRETCHES, STRETCHES, G_DEV)[:, :, :PER_SRC]
    block_ids = owner_ids[None, :, None] * G_DEV + shuffled
    start_slot = jnp.cumsum(counts, axis=1) - counts
    slot_pos = start_slot[:, :, None] + jnp.arange(PER_SRC)[None, None, :]
    is_live = jnp.arange(PER_SRC)[None, None, :] < counts[:, :, None]
    slot_pos = jnp.where(is_live, slot_pos, LIST)
    row_ids = jnp.broadcast_to(jnp.arange(STRETCHES)[:, None, None], slot_pos.shape)
    padded_table = jnp.zeros((STRETCHES, LIST + 1), jnp.int32).at[row_ids, slot_pos].set(block_ids.astype(jnp.int32))
    return (padded_table[:, :LIST], jnp.sum(counts, axis=1).astype(jnp.int32))


def draw_block_list(key, part):
    shared = list_parts(key)
    return shared[0]


def draw_list_len(key, part):
    shared = list_parts(key)
    return shared[1]


def draw_tok_count(key, part):
    key = jax.random.fold_in(key, 21)
    counts = jax.random.randint(jax.random.fold_in(key, 1), (STRETCHES,), STRETCH_TOK // 2, STRETCH_TOK + 1)
    full_stretch = jax.random.randint(jax.random.fold_in(key, 2), (), 0, STRETCHES)
    return jnp.where(jnp.arange(STRETCHES) == full_stretch, STRETCH_TOK, counts).astype(jnp.int32)


def draw_queries(key, part):
    key = jax.random.fold_in(key, 31)
    full_shape = (STRETCHES, STRETCH_TOK, HEADS * HEAD_DIM)
    drawn = jnp.clip(jax.random.normal(key, full_shape, jnp.float32), -4.0, 4.0)
    return drawn.astype(jnp.bfloat16)


def draw_stretch_keys(key, part):
    key = jax.random.fold_in(key, 41)
    full_shape = (STRETCHES, STRETCH_TOK, HEADS * HEAD_DIM)
    drawn = jnp.clip(jax.random.normal(key, full_shape, jnp.float32), -4.0, 4.0)
    return drawn.astype(jnp.bfloat16)


def with_ends(result, key, low, largest):
    longest = result.shape.index(max(result.shape))
    spots = []
    for shift in (0, 1):
        where = [jax.random.randint(jax.random.fold_in(key, axis), (), 0, length) for axis, length in enumerate(result.shape)]
        where[longest] = (where[longest] + shift) % result.shape[longest]
        spots.append(tuple(where))
    return result.at[spots[0]].set(low).at[spots[1]].set(largest)


def shard_levels(key, shape, pieces, least, high):
    level, own = 1.0, jax.random.fold_in(key, 6)
    for axis_at, blocks in pieces:
        draws = jnp.exp(jax.random.uniform(jax.random.fold_in(own, axis_at), (blocks,), jnp.float32, least / len(pieces), high / len(pieces)))
        level = level * jnp.repeat(draws, shape[axis_at] // blocks).reshape([-1 if axis == axis_at else 1 for axis in range(len(shape))])
    return level


def gaussian(rng, shape, deviation, reach, pieces=(), kind=jnp.bfloat16):
    factor_of = shard_levels(rng, shape, pieces, -0.22, 0.18) if pieces else 1.0
    result = jax.random.normal(rng, shape, jnp.float32) * deviation * factor_of
    return jnp.minimum(jnp.maximum(result, -reach), reach).astype(kind)


def setup_inputs(seed: int = 0) -> dict:
    arg_keys = jax.random.split(jax.random.key(seed), 11)
    queries = draw_queries(jax.random.fold_in(arg_keys[10], 71), 0)
    stretch_keys = draw_stretch_keys(jax.random.fold_in(arg_keys[10], 71), 0)
    stretch_values = gaussian(arg_keys[2], (STRETCHES, STRETCH_TOK, FEATURES), 1.0, 6.0, ((0, 4), (1, 64)))
    cache_keys = gaussian(arg_keys[3], (BLOCKS, STRETCH_TOK, FEATURES), 1.0, 4.0, ((0, 4), (1, 64)))
    cache_values = gaussian(arg_keys[4], (BLOCKS, STRETCH_TOK, FEATURES), 1.0, 6.0, ((0, 4), (1, 64)))
    block_list = draw_block_list(jax.random.fold_in(arg_keys[10], 71), 0)
    list_len = draw_list_len(jax.random.fold_in(arg_keys[10], 71), 0)
    tok_count = draw_tok_count(jax.random.fold_in(arg_keys[10], 71), 0)
    noise_levels = with_ends(jax.random.randint(arg_keys[8], (STRETCHES,), 0, LEVELS), jax.random.fold_in(arg_keys[8], 1), 0, LEVELS - 1).astype(jnp.int32)
    gate_table = jnp.clip(1.0 + 0.18 * jax.random.normal(arg_keys[9], (LEVELS, FEATURES), jnp.float32), 0.1, 1.9)
    return {"queries": queries, "stretch_keys": stretch_keys, "stretch_values": stretch_values, "cache_keys": cache_keys, "cache_values": cache_values, "block_list": block_list, "list_len": list_len, "tok_count": tok_count, "noise_levels": noise_levels, "gate_table": gate_table}


MASKED_SCORE = -1e+30

def attend_stretch(query_rows, key_rows, value_rows, keep_mask):
    score_scale = 1.0 / math.sqrt(HEAD_DIM)

    def one_head(head_parts):
        q_head, k_head, v_head = head_parts
        scores = jnp.dot(q_head, k_head.T, preferred_element_type=jnp.float32) * score_scale
        scores = jnp.where(keep_mask[None, :], scores, MASKED_SCORE)
        row_max = lax.optimization_barrier(jnp.max(scores, axis=1, keepdims=True))
        weights = jnp.where(keep_mask[None, :], jnp.exp(scores - row_max), 0.0)
        row_total = lax.optimization_barrier(jnp.sum(weights, axis=1, keepdims=True))
        attended = jnp.dot(weights.astype(jnp.bfloat16), v_head, preferred_element_type=jnp.float32)
        return attended / row_total
    return lax.map(one_head, (query_rows.transpose(1, 0, 2), key_rows.transpose(1, 0, 2), value_rows.transpose(1, 0, 2)))

def reference(queries, stretch_keys, stretch_values, cache_keys, cache_values, block_list, list_len, tok_count, noise_levels, gate_table):
    results = []
    for stretch_idx in range(STRETCHES):
        picked = block_list[stretch_idx]
        key_rows = jnp.concatenate([stretch_keys[stretch_idx][None], cache_keys[picked]], axis=0).reshape(-1, HEADS, HEAD_DIM)
        value_rows = jnp.concatenate([stretch_values[stretch_idx][None], cache_values[picked]], axis=0).reshape(-1, HEADS, HEAD_DIM)
        own_keep = jnp.arange(STRETCH_TOK) < tok_count[stretch_idx]
        entry_keep = jnp.arange(picked.shape[0]) < list_len[stretch_idx]
        keep_mask = jnp.concatenate([own_keep, jnp.repeat(entry_keep, STRETCH_TOK)])
        query_rows = queries[stretch_idx].reshape(STRETCH_TOK, HEADS, HEAD_DIM)
        attended = attend_stretch(query_rows, key_rows, value_rows, keep_mask).transpose(1, 0, 2)
        normed = attended * lax.rsqrt(lax.optimization_barrier(jnp.mean(attended * attended, axis=2, keepdims=True)) + 1e-06)
        gated_rows = normed.reshape(STRETCH_TOK, HEADS * HEAD_DIM) * gate_table[noise_levels[stretch_idx]][None, :]
        results.append(jnp.where(own_keep[:, None], gated_rows, 0.0).astype(jnp.bfloat16))
    return jnp.roll(jnp.stack(results), 1, axis=0)
```

```python
import functools
import math

import jax
import jax.numpy as jnp
from jax import lax
from jax.experimental import pallas as pl
from jax.experimental.pallas import tpu as pltpu
from jax.sharding import Mesh
from jax.sharding import PartitionSpec as P

HEAD_DIM = 128
LOCAL_HEADS = 3
COLS = LOCAL_HEADS * HEAD_DIM
PER_SRC = 4
MEMBERS = 8
ROWS = 16
CLEAN = 8
MASKED = -1e30
UNUSED = 1e30
LOG2E = 1.4426950408889634
KEYS = 256
AXES = ("zh", "x", "yh", "yl", "zl", "core")
OFFSETS = [(dx, dy) for dx in (2, 1, 3, 0) for dy in (1, 0) if (dx, dy) != (0, 0)]


class Place:
    def __init__(self):
        for name in AXES:
            setattr(self, name, lax.axis_index(name))
        self.z = self.zh * 2 + self.zl
        self.member = self.x * 2 + self.yl

    def peer(self, dx, dy):
        return (self.x + dx) % 4, (self.yl + dy) % 2

    def to_peer(self, dx, dy):
        px, py = self.peer(dx, dy)
        return {"x": px, "yl": py}

    def to_z(self, step):
        other = (self.z + step + 8) % 8
        return {"zh": other // 2, "zl": other % 2}

    def to_y(self):
        return {"yh": 1 - self.yh}

    def to_core(self):
        return {"core": 1 - self.core}


def greet(targets):
    barrier = pltpu.get_barrier_semaphore()
    for target in targets:
        pl.semaphore_signal(barrier, inc=1, device_id=target, device_id_type=pl.DeviceIdType.MESH)
    pl.semaphore_wait(barrier, len(targets))


def remote(src, dst, send, recv, target):
    return pltpu.make_async_remote_copy(
        src_ref=src, dst_ref=dst, send_sem=send, recv_sem=recv, device_id=target, device_id_type=pl.DeviceIdType.MESH
    )


def spread_kernel(
    q, sk, sv, ck, cv, keys, values, queries, kv_send, kv_recv, q_send, q_recv, core_send, core_recv,
    up_send, up_recv, down_send, down_recv, y_send, y_recv, local,
):
    at = Place()
    greet([at.to_peer(*off) for off in OFFSETS] + [at.to_z(1), at.to_z(-1), at.to_y(), at.to_core()])

    def slot(member):
        return pl.ds(pl.multiple_of((at.core * 8 + member) * ROWS, ROWS), ROWS)

    def columns(member):
        return pl.ds(pl.multiple_of(member * COLS, COLS), COLS)

    mine = slot(at.member)
    q_row = pl.ds(pl.multiple_of(at.yh * 128 + at.member * ROWS, ROWS), ROWS)
    q_copies = []
    for n, off in enumerate(OFFSETS):
        px, py = at.peer(*off)
        copy = remote(
            q.at[0, :, columns(px * 2 + py)], queries.at[at.z, q_row, :], q_send.at[n], q_recv.at[n], at.to_peer(*off)
        )
        copy.start()
        q_copies.append(copy)
    q_own = pltpu.make_async_copy(q.at[0, :, columns(at.member)], queries.at[at.z, q_row, :], local.at[4])
    q_own.start()
    own = [
        pltpu.make_async_copy(ck.at[:, :, columns(at.member)], keys.at[pl.ds(0, CLEAN), mine, :], local.at[0]),
        pltpu.make_async_copy(cv.at[:, :, columns(at.member)], values.at[pl.ds(0, CLEAN), mine, :], local.at[1]),
        pltpu.make_async_copy(sk.at[:, :, columns(at.member)], keys.at[pl.ds(CLEAN, 1), mine, :], local.at[2]),
        pltpu.make_async_copy(sv.at[:, :, columns(at.member)], values.at[pl.ds(CLEAN, 1), mine, :], local.at[3]),
    ]
    for copy in own:
        copy.start()
    kv_copies = []
    for n, off in enumerate(OFFSETS):
        px, py = at.peer(*off)
        cols = columns(px * 2 + py)
        target = at.to_peer(*off)
        group = [
            remote(ck.at[:, :, cols], keys.at[pl.ds(0, CLEAN), mine, :], kv_send.at[n, 0], kv_recv.at[n, 0], target),
            remote(cv.at[:, :, cols], values.at[pl.ds(0, CLEAN), mine, :], kv_send.at[n, 1], kv_recv.at[n, 1], target),
            remote(sk.at[:, :, cols], keys.at[pl.ds(CLEAN, 1), mine, :], kv_send.at[n, 2], kv_recv.at[n, 2], target),
            remote(sv.at[:, :, cols], values.at[pl.ds(CLEAN, 1), mine, :], kv_send.at[n, 3], kv_recv.at[n, 3], target),
        ]
        for copy in group:
            copy.start()
        kv_copies.append(group)

    forwards = []

    def forward(n, member):
        where = slot(member)
        for part, ref in enumerate((keys, values)):
            copy = remote(
                ref.at[:, where, :], ref.at[:, where, :], core_send.at[n, part], core_recv.at[n, part], at.to_core()
            )
            copy.start()
            forwards.append(copy)

    def forward_received(n):
        for copy in kv_copies[n]:
            copy.wait_recv()
        dx, dy = OFFSETS[n]
        px, py = at.peer(-dx + 4, dy)
        forward(n, px * 2 + py)

    def half(plane, r):
        which = (at.yh + r) % 2
        return queries.at[plane, pl.ds(pl.multiple_of(which * 128, 128), 128), :]

    ring = {}

    def ring_start(up, step, r):
        plane = (at.z - step + 8) % 8 if up else (at.z + step) % 8
        send, recv = (up_send, up_recv) if up else (down_send, down_recv)
        part = half(plane, r)
        copy = remote(part, part, send.at[step, r], recv.at[step, r], at.to_z(1 if up else -1))
        copy.start()
        ring[up, step, r] = copy

    q_own.wait()
    for copy in q_copies:
        copy.wait_recv()
    y_copy = remote(half(at.z, 0), half(at.z, 0), y_send, y_recv, at.to_y())
    y_copy.start()
    ring_start(True, 0, 0)
    ring_start(False, 0, 0)
    y_copy.wait_recv()
    ring_start(True, 0, 1)
    ring_start(False, 0, 1)
    for copy in own:
        copy.wait()
    forward(7, at.member)
    order = [5, 6, 1, 3, 0, 2, 4]
    order = [n for n in range(7)][::-1]
    todo = list(order)
    for step in (1, 2, 3):
        for r in (0, 1):
            ring[True, step - 1, r].wait_recv()
            if step < 3 or r == 0:
                ring_start(True, step, r)
            ring[False, step - 1, r].wait_recv()
            if step < 3 or r == 1:
                ring_start(False, step, r)
        forward_received(todo.pop(0))
    while todo:
        forward_received(todo.pop(0))
    ring[True, 3, 0].wait_recv()
    ring[False, 3, 1].wait_recv()
    for copy in forwards:
        copy.wait_recv()
    for copy in forwards:
        copy.wait_send()
    for copy in ring.values():
        copy.wait_send()
    y_copy.wait_send()
    for copy in q_copies:
        copy.wait_send()
    for group in kv_copies:
        for copy in group:
            copy.wait_send()


def spread(q, sk, sv, ck, cv):
    hbm = pl.BlockSpec(memory_space=pl.ANY)
    dma = pltpu.SemaphoreType.DMA
    return pl.pallas_call(
        spread_kernel,
        out_shape=(
            jax.ShapeDtypeStruct((CLEAN + 1, KEYS, COLS), jnp.bfloat16),
            jax.ShapeDtypeStruct((CLEAN + 1, KEYS, COLS), jnp.bfloat16),
            jax.ShapeDtypeStruct((8, 256, COLS), jnp.bfloat16),
        ),
        in_specs=[hbm] * 5,
        out_specs=(hbm,) * 3,
        scratch_shapes=[
            dma((7, 4)), dma((7, 4)), dma((7,)), dma((7,)), dma((8, 2)), dma((8, 2)),
            dma((4, 2)), dma((4, 2)), dma((4, 2)), dma((4, 2)), dma, dma, dma((5,)),
        ],
        compiler_params=pltpu.CompilerParams(collective_id=0, has_side_effects=True),
    )(q, sk, sv, ck, cv)


def pick_blocks(block_list, list_len, stretch, owner):
    zero = jnp.int32(0)
    picked = [zero] * PER_SRC
    count = zero
    for entry in range(16):
        block = block_list[stretch, entry]
        mine = jnp.logical_and(block // CLEAN == owner, entry < list_len[stretch])
        for e in range(PER_SRC):
            picked[e] = jnp.where(jnp.logical_and(mine, count == e), block % CLEAN, picked[e])
        count = count + jnp.where(mine, 1, 0)
    return picked, count


def attend_kernel(block_list, list_len, tok_count, keys, values, queries, sums, stats, turned):
    at = Place()
    scale = LOG2E / math.sqrt(HEAD_DIM)

    def turn(block, carry):
        turned[block] = values[block].T
        return carry

    lax.fori_loop(0, CLEAN + 1, turn, 0)

    def unit(plane, carry):
        stretch = plane // 2
        dest = (plane + 2) % 8
        picked, count = pick_blocks(block_list, list_len, stretch, at.zh)

        def heads(with_own):
            def head(h, inner):
                lanes = pl.ds(pl.multiple_of(h * HEAD_DIM, HEAD_DIM), HEAD_DIM)
                q_head = queries[plane, :, lanes]
                score_parts, live, turned_parts = [], [], []
                for e in range(PER_SRC):
                    score_parts.append(
                        lax.dot_general(
                            keys[picked[e], :, lanes], q_head, (((1,), (1,)), ((), ())),
                            preferred_element_type=jnp.float32,
                        )
                    )
                    live.append(e < count)
                    turned_parts.append(turned[picked[e], lanes, :])
                if with_own:
                    own_scores = lax.dot_general(
                        keys[CLEAN, :, lanes], q_head, (((1,), (1,)), ((), ())), preferred_element_type=jnp.float32
                    )
                    j = lax.broadcasted_iota(jnp.int32, own_scores.shape, 0)
                    position = (
                        ((j // 32) % 4) * 256 + at.yh * 128 + ((j // 16) % 2) * 64 + at.zl * 32 + (j // 128) * 16 + j % 16
                    )
                    own_scores = jnp.where(position < tok_count[stretch], own_scores, MASKED)
                    score_parts.append(own_scores)
                    live.append(None)
                    turned_parts.append(turned[CLEAN, lanes, :])
                top = None
                for part, ok in zip(score_parts, live):
                    part_top = jnp.max(part, axis=0, keepdims=True)
                    if ok is not None:
                        part_top = jnp.where(ok, part_top, MASKED)
                    top = part_top if top is None else jnp.maximum(top, part_top)
                shift = top * scale
                total = None
                weight_parts = []
                for part, ok in zip(score_parts, live):
                    if ok is not None:
                        offset = jnp.where(ok, shift, UNUSED)
                    else:
                        offset = jnp.where(top > 0.5 * MASKED, shift, UNUSED)
                    weights = jnp.exp2(part * scale - offset)
                    part_total = jnp.sum(weights, axis=0, keepdims=True)
                    total = part_total if total is None else total + part_total
                    weight_parts.append(weights.astype(jnp.bfloat16))
                product = jnp.dot(
                    jnp.concatenate(turned_parts, axis=1),
                    jnp.concatenate(weight_parts, axis=0),
                    preferred_element_type=jnp.float32,
                )
                sums[dest, lanes, :] = product.astype(jnp.bfloat16)
                stats[dest, pl.ds(h, 1), :] = shift
                stats[dest, pl.ds(h + LOCAL_HEADS, 1), :] = total
                return inner

            lax.fori_loop(0, LOCAL_HEADS, head, 0)
            stats[dest, pl.ds(2 * LOCAL_HEADS, 2), :] = jnp.zeros((2, 256), jnp.float32)

        @pl.when(stretch == at.zh)
        def _():
            heads(True)

        @pl.when(stretch != at.zh)
        def _():
            heads(False)

        return carry

    lax.fori_loop(0, 8, unit, 0)


def attend(block_list, list_len, tok_count, keys, values, queries):
    smem = pl.BlockSpec(memory_space=pltpu.SMEM)
    vmem = pl.BlockSpec(memory_space=pltpu.VMEM)
    return pl.pallas_call(
        attend_kernel,
        out_shape=(
            jax.ShapeDtypeStruct((8, COLS, 256), jnp.bfloat16),
            jax.ShapeDtypeStruct((8, 8, 256), jnp.float32),
        ),
        in_specs=[smem] * 3 + [vmem] * 3,
        out_specs=(vmem, vmem),
        scratch_shapes=[pltpu.VMEM((CLEAN + 1, COLS, KEYS), jnp.bfloat16)],
        compiler_params=pltpu.CompilerParams(vmem_limit_bytes=48 * 1024 * 1024),
    )(block_list, list_len, tok_count, keys, values, queries)


def merge(parts):
    tops = [stat[0:LOCAL_HEADS] for _, stat in parts]
    top = functools.reduce(jnp.maximum, tops)
    factors = [jnp.exp2(t - top) for t in tops]
    total = functools.reduce(jnp.add, [f * stat[LOCAL_HEADS : 2 * LOCAL_HEADS] for f, (_, stat) in zip(factors, parts)])
    sums = []
    for h in range(LOCAL_HEADS):
        rows = slice(h * HEAD_DIM, (h + 1) * HEAD_DIM)
        sums.append(
            functools.reduce(
                jnp.add, [s[rows].astype(jnp.float32) * f[h : h + 1] for f, (s, _) in zip(factors, parts)]
            )
        )
    return sums, top, total


def join_kernel(
    tok_count, noise_levels, sums, stats, gate_table, out, held, held_stats, got, got_stats, y_got, y_stats, gates, ready,
    s_send, s_recv, t_send, t_recv, y_send, y_recv, out_send, out_recv, local,
):
    at = Place()
    greet([at.to_peer(*off) for off in OFFSETS] + [at.to_z(1), at.to_z(-1), at.to_y()])
    stretch = (at.zh + 3) % 4
    my_columns = pl.ds(pl.multiple_of(at.member * COLS, COLS), COLS)
    gate_copy = pltpu.make_async_copy(gate_table.at[:, my_columns], gates, local.at[0])
    gate_copy.start()
    copies = []
    for step in range(4):
        for side in (0, 1):
            dest = (at.z + 4 + step) % 8 if side == 0 else (at.z + 4 - step) % 8
            lanes = pl.ds(side * 128, 128) if step == 0 else pl.ds(0, 256)
            if step == 0:
                src, src_stats = sums.at[dest, :, lanes], stats.at[dest, :, lanes]
            else:
                copies[(step - 1) * 4 + side * 2].wait_recv()
                copies[(step - 1) * 4 + side * 2 + 1].wait_recv()
                if step == 1:
                    here = slice(side * 128, side * 128 + 128)
                    there = slice((1 - side) * 128, (1 - side) * 128 + 128)
                    held[step, side, :, there] = sums[dest, :, there]
                    held_stats[step, side, :, there] = stats[dest, :, there]
                else:
                    here = slice(0, 256)
                merged, top, total = merge(
                    [
                        (sums[dest, :, here], stats[dest, :, here]),
                        (got[step - 1, side, :, here], got_stats[step - 1, side, :, here]),
                    ]
                )
                for h in range(LOCAL_HEADS):
                    held[step, side, h * HEAD_DIM : (h + 1) * HEAD_DIM, here] = merged[h].astype(jnp.bfloat16)
                held_stats[step, side, 0:LOCAL_HEADS, here] = top
                held_stats[step, side, LOCAL_HEADS : 2 * LOCAL_HEADS, here] = total
                src, src_stats = held.at[step, side, :, lanes], held_stats.at[step, side, :, lanes]
            target = at.to_z(-1 if side == 0 else 1)
            pair = [
                remote(src, got.at[step, side, :, lanes], s_send.at[step, side], s_recv.at[step, side], target),
                remote(src_stats, got_stats.at[step, side, :, lanes], t_send.at[step, side], t_recv.at[step, side], target),
            ]
            for copy in pair:
                copy.start()
            copies += pair
    for copy in copies[-4:]:
        copy.wait_recv()

    def my_parts(lanes):
        return [
            (sums[at.z, :, lanes], stats[at.z, :, lanes]),
            (got[3, 0, :, lanes], got_stats[3, 0, :, lanes]),
            (got[3, 1, :, lanes], got_stats[3, 1, :, lanes]),
        ]

    other = pl.ds(pl.multiple_of((1 - at.yh) * 128, 128), 128)
    mine = pl.ds(pl.multiple_of(at.yh * 128, 128), 128)
    merged, top, total = merge(my_parts(other))
    for h in range(LOCAL_HEADS):
        held[0, 0, h * HEAD_DIM : (h + 1) * HEAD_DIM, 0:128] = merged[h].astype(jnp.bfloat16)
    held_stats[0, 0, 0:LOCAL_HEADS, 0:128] = top
    held_stats[0, 0, LOCAL_HEADS : 2 * LOCAL_HEADS, 0:128] = total
    y_pair = [
        remote(held.at[0, 0, :, pl.ds(0, 128)], y_got, y_send.at[0], y_recv.at[0], at.to_y()),
        remote(held_stats.at[0, 0, :, pl.ds(0, 128)], y_stats, y_send.at[1], y_recv.at[1], at.to_y()),
    ]
    for copy in y_pair:
        copy.start()
    gate_copy.wait()
    gate_row = gates[pl.ds(noise_levels[stretch], 1), :]
    r = lax.broadcasted_iota(jnp.int32, (128, HEAD_DIM), 0)
    position = (r // 32) * 256 + at.yh * 128 + ((r // 16) % 2) * 64 + at.zl * 32 + at.core * 16 + r % 16
    keep = position < tok_count[stretch]
    for copy in y_pair:
        copy.wait_recv()
    merged, top, total = merge(my_parts(mine) + [(y_got[...], y_stats[...])])
    for h in range(LOCAL_HEADS):
        attended = merged[h] / total[h : h + 1]
        mean_sq = jnp.mean(attended * attended, axis=0, keepdims=True)
        normed = (attended * lax.rsqrt(mean_sq + 1e-6)).T
        gated = jnp.where(keep, normed * gate_row[:, h * HEAD_DIM : (h + 1) * HEAD_DIM], 0.0)
        ready[:, h * HEAD_DIM : (h + 1) * HEAD_DIM] = gated.astype(jnp.bfloat16)
    outs = []
    for n, off in enumerate(OFFSETS):
        px, py = at.peer(*off)
        rows = pl.ds(pl.multiple_of((px * 2 + py) * ROWS, ROWS), ROWS)
        copy = remote(ready.at[rows, :], out.at[0, :, my_columns], out_send.at[n], out_recv.at[n], at.to_peer(*off))
        copy.start()
        outs.append(copy)
    rows = pl.ds(pl.multiple_of(at.member * ROWS, ROWS), ROWS)
    keep_copy = pltpu.make_async_copy(ready.at[rows, :], out.at[0, :, my_columns], local.at[1])
    keep_copy.start()
    for copy in copies + y_pair:
        copy.wait_send()
    keep_copy.wait()
    for copy in outs:
        copy.wait()


def join(tok_count, noise_levels, sums, stats, gate_table):
    smem = pl.BlockSpec(memory_space=pltpu.SMEM)
    vmem = pl.BlockSpec(memory_space=pltpu.VMEM)
    hbm = pl.BlockSpec(memory_space=pl.ANY)
    dma = pltpu.SemaphoreType.DMA
    return pl.pallas_call(
        join_kernel,
        out_shape=jax.ShapeDtypeStruct((1, ROWS, MEMBERS * COLS), jnp.bfloat16),
        in_specs=[smem, smem, vmem, vmem, hbm],
        out_specs=hbm,
        scratch_shapes=[
            pltpu.VMEM((4, 2, COLS, 256), jnp.bfloat16),
            pltpu.VMEM((4, 2, 8, 256), jnp.float32),
            pltpu.VMEM((4, 2, COLS, 256), jnp.bfloat16),
            pltpu.VMEM((4, 2, 8, 256), jnp.float32),
            pltpu.VMEM((COLS, 128), jnp.bfloat16),
            pltpu.VMEM((8, 128), jnp.float32),
            pltpu.VMEM((48, COLS), jnp.float32),
            pltpu.VMEM((128, COLS), jnp.bfloat16),
            dma((4, 2)), dma((4, 2)), dma((4, 2)), dma((4, 2)), dma((2,)), dma((2,)), dma((7,)), dma((7,)), dma((2,)),
        ],
        compiler_params=pltpu.CompilerParams(
            collective_id=1, has_side_effects=True, vmem_limit_bytes=48 * 1024 * 1024
        ),
    )(tok_count, noise_levels, sums, stats, gate_table)


def shards(q, sk, sv, ck, cv, block_list, list_len, tok_count, noise_levels, gate_table):
    keys, values, queries = spread(q, sk, sv, ck, cv)
    sums, stats = attend(block_list, list_len, tok_count, keys, values, queries)
    return join(tok_count, noise_levels, sums, stats, gate_table)


def solution(mesh):
    fine = Mesh(mesh.devices.reshape(4, 4, 2, 2, 2, 2), AXES)
    split = P("zh", ("x", "yh", "yl", "zl", "core"), None)
    return jax.shard_map(
        shards, mesh=fine, in_specs=(split,) * 5 + (P(),) * 5, out_specs=split, check_vma=False
    )
```

```python
import functools
import math

import jax
import jax.numpy as jnp
from jax import lax
from jax.experimental import pallas as pl
from jax.experimental.pallas import tpu as pltpu
from jax.sharding import Mesh
from jax.sharding import PartitionSpec as P

HEAD_DIM = 128
LOCAL_HEADS = 3
COLS = LOCAL_HEADS * HEAD_DIM
PER_SRC = 4
MEMBERS = 8
ROWS = 16
CLEAN = 8
LIST = 16
STRETCHES = 4
KEYS = 256
QUERIES = 256
MASKED = -1e30
UNUSED = 1e30
SCALE = 1.4426950408889634 / math.sqrt(HEAD_DIM)
AXES = ("zh", "x", "yh", "yl", "zl", "core")
GROUP = [(dx, dl) for dx in (2, 1, 3, 0) for dl in (1, 0) if (dx, dl) != (0, 0)]
PLANE = [(dx, dh, dl) for dx in (2, 1, 3, 0) for dh in (1, 0) for dl in (1, 0) if (dx, dh, dl) != (0, 0, 0)]


class Place:
    def __init__(self):
        for name in AXES:
            setattr(self, name, lax.axis_index(name))
        self.z = self.zh * 2 + self.zl
        self.member = self.x * 2 + self.yl

    def peer(self, dx, dl):
        px, pyl = (self.x + dx) % 4, (self.yl + dl) % 2
        return {"x": px, "yl": pyl}, px * 2 + pyl

    def in_plane(self, dx, dh, dl):
        target, member = self.peer(dx, dl)
        return dict(target, yh=(self.yh + dh) % 2), member

    def to_z(self, step):
        other = (self.z + step + 8) % 8
        return {"zh": other // 2, "zl": other % 2}

    def to_y(self):
        return {"yh": 1 - self.yh}

    def to_core(self):
        return {"core": 1 - self.core}


def greet(targets):
    barrier = pltpu.get_barrier_semaphore()
    for target in targets:
        pl.semaphore_signal(barrier, inc=1, device_id=target, device_id_type=pl.DeviceIdType.MESH)
    pl.semaphore_wait(barrier, len(targets))


def remote(src, dst, send, recv, target):
    return pltpu.make_async_remote_copy(
        src_ref=src, dst_ref=dst, send_sem=send, recv_sem=recv, device_id=target, device_id_type=pl.DeviceIdType.MESH
    )


def drain(ref, sem):
    pltpu.make_async_copy(ref, ref, sem).wait()


def aligned(start, size):
    return pl.ds(pl.multiple_of(start, size), size)


def merge(parts):
    top = functools.reduce(jnp.maximum, [t for _, t, _ in parts])
    factors = [jnp.exp2(t - top) for _, t, _ in parts]
    total = functools.reduce(jnp.add, [f * n for f, (_, _, n) in zip(factors, parts)])
    sums = functools.reduce(jnp.add, [s.astype(jnp.float32) * f for f, (s, _, _) in zip(factors, parts)])
    return sums, top, total


def read_stats(ref):
    tile = ref[...]
    return [(tile[i : i + 1], tile[2 + i : 3 + i]) for i in (0, 1)]


def write_stats(ref, half, top, total):
    ref[half : half + 1, :] = top
    ref[2 + half : 3 + half, :] = total


def kernel(
    block_list, list_len, tok_count, noise_levels, q, sk, sv, ck, cv, gate_table, out,
    keys0, keys1, keys2, values0, values1, values2, turned, queries, own_bias, picked,
    sums, stats, held, held_stats, got, got_stats, y_held, y_held_stats, y_got, y_got_stats, gates, ready,
    kv_send, kv_recv, core_send, core_recv, q_send, q_recv, ring_send, ring_recv,
    p_send, p_recv, t_send, t_recv, y_send, y_recv, out_send, out_recv, gate_sem,
):
    at = Place()
    keys, values = (keys0, keys1, keys2), (values0, values1, values2)
    greet([at.in_plane(*off)[0] for off in PLANE] + [at.to_z(1), at.to_z(-1), at.to_core()])

    q_rows = aligned(at.yh * 128 + at.member * ROWS, ROWS)
    q_dst = queries.at[at.z, q_rows, :]
    for off in PLANE:
        target, member = at.in_plane(*off)
        remote(q.at[0, :, aligned(member * COLS, COLS)], q_dst, q_send, q_recv, target).start()
    pltpu.make_async_copy(q.at[0, :, aligned(at.member * COLS, COLS)], q_dst, q_recv).start()

    slot = aligned((at.core * MEMBERS + at.member) * ROWS, ROWS)
    my_half = aligned(at.core * 128, 128)

    def send_keys(h):
        for part, (cached, own, ref) in enumerate(((ck, sk, keys[h]), (cv, sv, values[h]))):
            cached_dst, own_dst = ref.at[pl.ds(0, CLEAN), slot, :], ref.at[pl.ds(CLEAN, 1), slot, :]
            for off in GROUP:
                target, member = at.peer(*off)
                cols = aligned(member * COLS + h * HEAD_DIM, HEAD_DIM)
                remote(cached.at[:, :, cols], cached_dst, kv_send.at[h, part], kv_recv.at[h, part], target).start()
                remote(own.at[:, :, cols], own_dst, kv_send.at[h, part], kv_recv.at[h, part], target).start()
            cols = aligned(at.member * COLS + h * HEAD_DIM, HEAD_DIM)
            pltpu.make_async_copy(cached.at[:, :, cols], cached_dst, kv_recv.at[h, part]).start()
            pltpu.make_async_copy(own.at[:, :, cols], own_dst, kv_recv.at[h, part]).start()

    def share_copy(h, part):
        ref = (keys[h], values[h])[part].at[:, my_half, :]
        return remote(ref, ref, core_send.at[h, part], core_recv.at[h, part], at.to_core())

    def share_keys(h):
        for part, ref in enumerate((keys[h], values[h])):
            drain(ref.at[:, my_half, :], kv_recv.at[h, part])
            share_copy(h, part).start()

    def take_keys(h):
        for part in (0, 1):
            share_copy(h, part).wait_recv()

        def turn(block, carry):
            turned[block] = values[h][block].T
            return carry

        lax.fori_loop(0, CLEAN + 1, turn, 0)

    def ring_copy(h, step, side):
        plane = (at.z - step + 8) % 8 if side == 0 else (at.z + step) % 8
        rows = pl.ds(side * 128, 128) if step == 3 else pl.ds(0, QUERIES)
        part = queries.at[plane, rows, pl.ds(h * HEAD_DIM, HEAD_DIM)]
        return remote(
            part, part, ring_send.at[h, step, side], ring_recv.at[h, step, side], at.to_z(1 if side == 0 else -1)
        )

    def ring_step(h, step):
        for side in (0, 1):
            if step > 0:
                ring_copy(h, step - 1, side).wait_recv()
            ring_copy(h, step, side).start()

    def ring_end(h):
        for side in (0, 1):
            ring_copy(h, 3, side).wait_recv()

    def dest_of(step, side):
        return (at.z + 4 + step) % 8 if side == 0 else (at.z + 4 - step) % 8

    def sum_copies(h, step, side):
        target = at.to_z(-1 if side == 0 else 1)
        dest = dest_of(step, side)
        if step == 0:
            lanes = pl.ds(side * 128, 128)
            src, src_stats = sums.at[h, dest, :, lanes], stats.at[h, dest]
        else:
            lanes = pl.ds(0, QUERIES)
            src, src_stats = held.at[h, step - 1, side], held_stats.at[h, step - 1, side]
        return [
            remote(src, got.at[h, step, side, :, lanes], p_send.at[h, step, side], p_recv.at[h, step, side], target),
            remote(src_stats, got_stats.at[h, step, side], t_send.at[h, step, side], t_recv.at[h, step, side], target),
        ]

    def sum_step(h, step):
        for side in (0, 1):
            if step > 0:
                for copy in sum_copies(h, step - 1, side):
                    copy.wait_recv()
                dest = dest_of(step, side)
                mine, theirs = read_stats(stats.at[h, dest]), read_stats(got_stats.at[h, step - 1, side])
                to_stats = held_stats.at[h, step - 1, side]
                for half in (0, 1):
                    lanes = slice(half * 128, half * 128 + 128)
                    if step == 1 and half != side:
                        held[h, 0, side, :, lanes] = sums[h, dest, :, lanes]
                        write_stats(to_stats, half, *mine[half])
                        continue
                    merged, top, total = merge(
                        [(sums[h, dest, :, lanes], *mine[half]), (got[h, step - 1, side, :, lanes], *theirs[half])]
                    )
                    held[h, step - 1, side, :, lanes] = merged.astype(jnp.bfloat16)
                    write_stats(to_stats, half, top, total)
            for copy in sum_copies(h, step, side):
                copy.start()

    def gathered(h, half):
        lanes = pl.ds(half * 128, 128)
        sources = [
            (sums.at[h, at.z], stats.at[h, at.z]),
            (got.at[h, 3, 0], got_stats.at[h, 3, 0]),
            (got.at[h, 3, 1], got_stats.at[h, 3, 1]),
        ]
        return [(ref[:, lanes], *read_stats(stat)[half]) for ref, stat in sources]

    def y_copies(h):
        return [
            remote(y_held.at[h], y_got.at[h], y_send.at[h, 0], y_recv.at[h, 0], at.to_y()),
            remote(y_held_stats.at[h], y_got_stats.at[h], y_send.at[h, 1], y_recv.at[h, 1], at.to_y()),
        ]

    def sum_end(h):
        for side in (0, 1):
            for copy in sum_copies(h, 3, side):
                copy.wait_recv()
        for half in (0, 1):

            @pl.when(at.yh != half)
            def _():
                merged, top, total = merge(gathered(h, half))
                y_held[h] = merged.astype(jnp.bfloat16)
                write_stats(y_held_stats.at[h], 0, top, total)

        for copy in y_copies(h):
            copy.start()

    stretch_out = (at.zh + 3) % 4

    def finish(h):
        for copy in y_copies(h):
            copy.wait_recv()
        r = lax.broadcasted_iota(jnp.int32, (128, HEAD_DIM), 0)
        position = (r // 32) * 256 + at.yh * 128 + ((r // 16) % 2) * 64 + at.zl * 32 + at.core * 16 + r % 16
        keep = position < tok_count[stretch_out]
        cols = pl.ds(h * HEAD_DIM, HEAD_DIM)
        gate_row = gates[pl.ds(noise_levels[stretch_out], 1), :][:, h * HEAD_DIM : (h + 1) * HEAD_DIM]
        for half in (0, 1):

            @pl.when(at.yh == half)
            def _():
                merged, top, total = merge(gathered(h, half) + [(y_got[h], *read_stats(y_got_stats.at[h])[0])])
                attended = merged / total
                mean_sq = jnp.mean(attended * attended, axis=0, keepdims=True)
                normed = (attended * lax.rsqrt(mean_sq + 1e-6)).T
                ready[:, cols] = jnp.where(keep, normed * gate_row, 0.0).astype(jnp.bfloat16)

        dst = out.at[0, :, aligned(at.member * COLS + h * HEAD_DIM, HEAD_DIM)]
        for off in GROUP:
            target, member = at.peer(*off)
            remote(ready.at[aligned(member * ROWS, ROWS), cols], dst, out_send.at[h], out_recv.at[h], target).start()
        pltpu.make_async_copy(ready.at[aligned(at.member * ROWS, ROWS), cols], dst, out_recv.at[h]).start()

    def unit(h, dest):
        plane = (dest + 6) % 8
        stretch = plane // 2
        cols = pl.ds(h * HEAD_DIM, HEAD_DIM)

        def run(with_own):
            q_head = queries[plane, :, cols]
            blocks = [picked[stretch, e] for e in range(PER_SRC)] + ([CLEAN] if with_own else [])
            scores = lax.dot_general(
                jnp.concatenate([keys[h][b] for b in blocks], axis=0), q_head, (((1,), (1,)), ((), ())),
                preferred_element_type=jnp.float32,
            )
            parts = [scores[n * KEYS : (n + 1) * KEYS] for n in range(len(blocks))]
            live = [e < picked[stretch, PER_SRC] for e in range(PER_SRC)]
            if with_own:
                bias = own_bias[...]
                parts[PER_SRC] = parts[PER_SRC] + jnp.concatenate([bias, bias], axis=1)
            top = jnp.full((1, QUERIES), MASKED, jnp.float32)
            for n, part in enumerate(parts):
                part_top = jnp.max(part, axis=0, keepdims=True)
                if n < PER_SRC:
                    part_top = jnp.where(live[n], part_top, MASKED)
                top = jnp.maximum(top, part_top)
            shift = top * SCALE
            total = jnp.zeros((1, QUERIES), jnp.float32)
            weights = []
            for n, part in enumerate(parts):
                offset = jnp.where(live[n], shift, UNUSED) if n < PER_SRC else shift
                weight = jnp.exp2(part * SCALE - offset)
                total = total + jnp.sum(weight, axis=0, keepdims=True)
                weights.append(weight.astype(jnp.bfloat16))
            product = jnp.dot(
                jnp.concatenate([turned[b] for b in blocks], axis=1), jnp.concatenate(weights, axis=0),
                preferred_element_type=jnp.float32,
            )
            sums[h, dest] = product.astype(jnp.bfloat16)
            for half in (0, 1):
                lanes = slice(half * 128, half * 128 + 128)
                write_stats(stats.at[h, dest], half, shift[:, lanes], total[:, lanes])

        pl.when(stretch == at.zh)(lambda: run(True))
        pl.when(stretch != at.zh)(lambda: run(False))

    gate_copy = pltpu.make_async_copy(gate_table.at[:, aligned(at.member * COLS, COLS)], gates, gate_sem)

    send_keys(0)
    drain(queries.at[at.z], q_recv)
    ring_step(0, 0)
    ring_step(1, 0)
    send_keys(1)
    gate_copy.start()
    for stretch in range(STRETCHES):
        count = jnp.int32(0)
        chosen = [jnp.int32(0)] * PER_SRC
        for entry in range(LIST):
            block = block_list[stretch, entry]
            hit = jnp.logical_and(block // CLEAN == at.zh, entry < list_len[stretch])
            for e in range(PER_SRC):
                chosen[e] = jnp.where(jnp.logical_and(hit, count == e), block % CLEAN, chosen[e])
            count = count + jnp.where(hit, 1, 0)
        for e in range(PER_SRC):
            picked[stretch, e] = chosen[e]
        picked[stretch, PER_SRC] = count
    ring_step(0, 1)
    ring_step(1, 1)
    j = lax.broadcasted_iota(jnp.int32, (KEYS, 128), 0)
    position = ((j // 32) % 4) * 256 + at.yh * 128 + ((j // 16) % 2) * 64 + at.zl * 32 + (j // 128) * 16 + j % 16
    own_bias[...] = jnp.where(position < tok_count[at.zh], 0.0, MASKED)
    send_keys(2)
    share_keys(0)
    ring_step(0, 2)
    ring_step(1, 2)
    take_keys(0)
    ring_step(0, 3)
    ring_step(1, 3)
    ring_step(2, 0)

    for h in range(LOCAL_HEADS):
        if h > 0:
            take_keys(h)
            ring_end(h)

        def body(u, carry):
            if h == 0:
                pl.when(u == 1)(lambda: ring_step(2, 1))
                pl.when(u == 3)(lambda: ring_step(2, 2))
                pl.when(u == 4)(lambda: ring_end(0))
                pl.when(u == 5)(lambda: ring_step(2, 3))
            if h + 1 < LOCAL_HEADS:
                pl.when(u == 4)(lambda: share_keys(h + 1))
            away = 4 - (u + 1) // 2
            dest = jnp.where(u % 2 == 1, at.z + away, at.z + 8 - away) % 8
            unit(h, dest)
            pl.when(u == 0)(lambda: sum_step(h, 0))
            for step in (1, 2, 3):
                pl.when(u == 2 * step)(functools.partial(sum_step, h, step))
            if h > 0:
                pl.when(u == 1)(lambda: finish(h - 1))
            return carry

        if h == 0:
            gate_copy.wait()
        lax.fori_loop(0, 8, body, 0)
        sum_end(h)
    finish(LOCAL_HEADS - 1)

    drain(queries.at[0, pl.ds(0, 15 * ROWS), :], q_send)
    for h in range(LOCAL_HEADS):
        for part, ref in enumerate((keys[h], values[h])):
            drain(ref.at[:, pl.ds(0, 7 * ROWS), :], kv_send.at[h, part])
            share_copy(h, part).wait_send()
        for side in (0, 1):
            for step in range(4):
                ring_copy(h, step, side).wait_send()
                for copy in sum_copies(h, step, side):
                    copy.wait_send()
        for copy in y_copies(h):
            copy.wait_send()
        drain(ready.at[pl.ds(0, 7 * ROWS), pl.ds(0, HEAD_DIM)], out_send.at[h])
        drain(out.at[0, :, pl.ds(0, MEMBERS * HEAD_DIM)], out_recv.at[h])


def shards(q, sk, sv, ck, cv, block_list, list_len, tok_count, noise_levels, gate_table):
    smem = pl.BlockSpec(memory_space=pltpu.SMEM)
    hbm = pl.BlockSpec(memory_space=pl.ANY)
    dma = pltpu.SemaphoreType.DMA
    bf, f32 = jnp.bfloat16, jnp.float32
    heads = LOCAL_HEADS
    return pl.pallas_call(
        kernel,
        out_shape=jax.ShapeDtypeStruct((1, ROWS, MEMBERS * COLS), bf),
        in_specs=[smem] * 4 + [hbm] * 6,
        out_specs=hbm,
        scratch_shapes=[pltpu.VMEM((CLEAN + 1, KEYS, HEAD_DIM), bf)] * 6
        + [
            pltpu.VMEM((CLEAN + 1, HEAD_DIM, KEYS), bf),
            pltpu.VMEM((8, QUERIES, COLS), bf),
            pltpu.VMEM((KEYS, 128), f32),
            pltpu.SMEM((STRETCHES, PER_SRC + 1), jnp.int32),
            pltpu.VMEM((heads, 8, HEAD_DIM, QUERIES), bf),
            pltpu.VMEM((heads, 8, 8, 128), f32),
            pltpu.VMEM((heads, 3, 2, HEAD_DIM, QUERIES), bf),
            pltpu.VMEM((heads, 3, 2, 8, 128), f32),
            pltpu.VMEM((heads, 4, 2, HEAD_DIM, QUERIES), bf),
            pltpu.VMEM((heads, 4, 2, 8, 128), f32),
            pltpu.VMEM((heads, HEAD_DIM, 128), bf),
            pltpu.VMEM((heads, 8, 128), f32),
            pltpu.VMEM((heads, HEAD_DIM, 128), bf),
            pltpu.VMEM((heads, 8, 128), f32),
            pltpu.VMEM((48, COLS), f32),
            pltpu.VMEM((128, COLS), bf),
            dma((heads, 2)), dma((heads, 2)), dma((heads, 2)), dma((heads, 2)), dma, dma,
            dma((heads, 4, 2)), dma((heads, 4, 2)), dma((heads, 4, 2)), dma((heads, 4, 2)),
            dma((heads, 4, 2)), dma((heads, 4, 2)), dma((heads, 2)), dma((heads, 2)), dma((heads,)), dma((heads,)), dma,
        ],
        compiler_params=pltpu.CompilerParams(
            collective_id=0, has_side_effects=True, vmem_limit_bytes=48 * 1024 * 1024
        ),
    )(block_list, list_len, tok_count, noise_levels, q, sk, sv, ck, cv, gate_table)


def solution(mesh):
    fine = Mesh(mesh.devices.reshape(4, 4, 2, 2, 2, 2), AXES)
    split = P("zh", ("x", "yh", "yl", "zl", "core"), None)
    return jax.shard_map(
        shards, mesh=fine, in_specs=(split,) * 5 + (P(),) * 5, out_specs=split, check_vma=False
    )
```

```python
import functools
import math

import jax
import jax.numpy as jnp
from jax import lax
from jax.experimental import pallas as pl
from jax.experimental.pallas import tpu as pltpu
from jax.sharding import Mesh
from jax.sharding import PartitionSpec as P

HEAD_DIM = 128
LOCAL_HEADS = 3
COLS = LOCAL_HEADS * HEAD_DIM
PER_SRC = 4
MEMBERS = 8
ROWS = 16
CLEAN = 8
LIST = 16
STRETCHES = 4
KEYS = 256
QUERIES = 256
MASKED = -1e30
UNUSED = 1e30
SCALE = 1.4426950408889634 / math.sqrt(HEAD_DIM)
AXES = ("zh", "x", "yh", "yl", "zl", "core")
GROUP = [(dx, dl) for dx in (2, 1, 3, 0) for dl in (1, 0) if (dx, dl) != (0, 0)]
PLANE = [(dx, dh, dl) for dx in (2, 1, 3, 0) for dh in (1, 0) for dl in (1, 0) if (dx, dh, dl) != (0, 0, 0)]


class Place:
    def __init__(self):
        for name in AXES:
            setattr(self, name, lax.axis_index(name))
        self.z = self.zh * 2 + self.zl
        self.member = self.x * 2 + self.yl

    def peer(self, dx, dl):
        px, pyl = (self.x + dx) % 4, (self.yl + dl) % 2
        return {"x": px, "yl": pyl}, px * 2 + pyl

    def in_plane(self, dx, dh, dl):
        target, member = self.peer(dx, dl)
        return dict(target, yh=(self.yh + dh) % 2), member

    def to_z(self, step):
        other = (self.z + step + 8) % 8
        return {"zh": other // 2, "zl": other % 2}

    def to_y(self):
        return {"yh": 1 - self.yh}

    def to_core(self):
        return {"core": 1 - self.core}


def greet(targets):
    barrier = pltpu.get_barrier_semaphore()
    for target in targets:
        pl.semaphore_signal(barrier, inc=1, device_id=target, device_id_type=pl.DeviceIdType.MESH)
    pl.semaphore_wait(barrier, len(targets))


def remote(src, dst, send, recv, target):
    return pltpu.make_async_remote_copy(
        src_ref=src, dst_ref=dst, send_sem=send, recv_sem=recv, device_id=target, device_id_type=pl.DeviceIdType.MESH
    )


def drain(ref, sem):
    pltpu.make_async_copy(ref, ref, sem).wait()


def aligned(start, size):
    return pl.ds(pl.multiple_of(start, size), size)


def dot_rows(a, b):
    return lax.dot_general(a, b, (((1,), (1,)), ((), ())), preferred_element_type=jnp.float32)


def merge(parts):
    top = functools.reduce(jnp.maximum, [t for _, t, _ in parts])
    factors = [jnp.exp2(t - top) for _, t, _ in parts]
    total = functools.reduce(jnp.add, [f * n for f, (_, _, n) in zip(factors, parts)])
    sums = functools.reduce(jnp.add, [s.astype(jnp.float32) * f for f, (s, _, _) in zip(factors, parts)])
    return sums, top, total


def read_stats(ref):
    tile = ref[...]
    return [(tile[i : i + 1], tile[2 + i : 3 + i]) for i in (0, 1)]


def write_stats(ref, half, top, total):
    ref[half : half + 1, :] = top
    ref[2 + half : 3 + half, :] = total


def kernel(
    block_list, list_len, tok_count, noise_levels, q, sk, sv, ck, cv, gate_table, out,
    keys0, keys1, keys2, values0, values1, values2, kept, turned, scores0, scores1, staged, stage_sem, queries, own_bias, picked,
    sums, stats, held, held_stats, got, got_stats, y_held, y_held_stats, y_got, y_got_stats, gates, ready,
    kv_send, kv_recv, core_send, core_recv, q_send, q_recv, ring_send, ring_recv,
    p_send, p_recv, t_send, t_recv, y_send, y_recv, out_send, out_recv, gate_sem,
):
    at = Place()
    keys, values = (keys0, keys1, keys2), (values0, values1, values2)
    staging = [
        pltpu.make_async_copy(ck, staged.at[0, pl.ds(0, CLEAN)], stage_sem.at[0]),
        pltpu.make_async_copy(cv, staged.at[1, pl.ds(0, CLEAN)], stage_sem.at[1]),
        pltpu.make_async_copy(sk, staged.at[0, pl.ds(CLEAN, 1)], stage_sem.at[2]),
        pltpu.make_async_copy(sv, staged.at[1, pl.ds(CLEAN, 1)], stage_sem.at[3]),
    ]
    for copy in staging:
        copy.start()
    greet([at.in_plane(*off)[0] for off in PLANE] + [at.to_z(1), at.to_z(-1), at.to_core()])

    q_rows = aligned(at.yh * 128 + at.member * ROWS, ROWS)
    q_dst = queries.at[at.z, q_rows, :]
    for off in PLANE:
        target, member = at.in_plane(*off)
        remote(q.at[0, :, aligned(member * COLS, COLS)], q_dst, q_send, q_recv, target).start()
    pltpu.make_async_copy(q.at[0, :, aligned(at.member * COLS, COLS)], q_dst, q_recv).start()

    slot = aligned((at.core * MEMBERS + at.member) * ROWS, ROWS)
    my_half = aligned(at.core * 128, 128)

    def send_keys(h):
        for part, ref in enumerate((keys[h], values[h])):
            dst = ref.at[:, slot, :]
            for off in GROUP:
                target, member = at.peer(*off)
                cols = aligned(member * COLS + h * HEAD_DIM, HEAD_DIM)
                remote(staged.at[part, :, :, cols], dst, kv_send.at[h, part], kv_recv.at[h, part], target).start()
            cols = aligned(at.member * COLS + h * HEAD_DIM, HEAD_DIM)
            pltpu.make_async_copy(staged.at[part, :, :, cols], dst, kv_recv.at[h, part]).start()

    def share_copy(h, part):
        ref = (keys[h], values[h])[part].at[:, my_half, :]
        return remote(ref, ref, core_send.at[h, part], core_recv.at[h, part], at.to_core())

    def share_keys(h):
        for part, ref in enumerate((keys[h], values[h])):
            drain(ref.at[:, my_half, :], kv_recv.at[h, part])
            share_copy(h, part).start()

    def take_keys(h):
        for part in (0, 1):
            share_copy(h, part).wait_recv()

        def turn(block, carry):
            kept[h, block] = keys[h][block]
            turned[h, block] = values[h][block].T
            return carry

        lax.fori_loop(0, CLEAN + 1, turn, 0)

    def ring_copy(h, step, side):
        plane = (at.z - step + 8) % 8 if side == 0 else (at.z + step) % 8
        rows = pl.ds(side * 128, 128) if step == 3 else pl.ds(0, QUERIES)
        piece = queries.at[plane, rows, pl.ds(h * HEAD_DIM, HEAD_DIM)]
        return remote(
            piece, piece, ring_send.at[h, step, side], ring_recv.at[h, step, side], at.to_z(1 if side == 0 else -1)
        )

    def ring_step(h, step):
        for side in (0, 1):
            if step > 0:
                ring_copy(h, step - 1, side).wait_recv()
            ring_copy(h, step, side).start()

    def ring_end(h):
        for side in (0, 1):
            ring_copy(h, 3, side).wait_recv()

    def dest_of(step, side):
        return (at.z + 4 + step) % 8 if side == 0 else (at.z + 4 - step) % 8

    def sum_copies(h, step, side):
        target = at.to_z(-1 if side == 0 else 1)
        dest = dest_of(step, side)
        if step == 0:
            lanes = pl.ds(side * 128, 128)
            src, src_stats = sums.at[h, dest, :, lanes], stats.at[h, dest]
        else:
            lanes = pl.ds(0, QUERIES)
            src, src_stats = held.at[h, step - 1, side], held_stats.at[h, step - 1, side]
        return [
            remote(src, got.at[h, step, side, :, lanes], p_send.at[h, step, side], p_recv.at[h, step, side], target),
            remote(src_stats, got_stats.at[h, step, side], t_send.at[h, step, side], t_recv.at[h, step, side], target),
        ]

    def sum_step(h, step):
        for side in (0, 1):
            if step > 0:
                for copy in sum_copies(h, step - 1, side):
                    copy.wait_recv()
                dest = dest_of(step, side)
                mine, theirs = read_stats(stats.at[h, dest]), read_stats(got_stats.at[h, step - 1, side])
                to_stats = held_stats.at[h, step - 1, side]
                for half in (0, 1):
                    lanes = slice(half * 128, half * 128 + 128)
                    if step == 1 and half != side:
                        held[h, 0, side, :, lanes] = sums[h, dest, :, lanes]
                        write_stats(to_stats, half, *mine[half])
                        continue
                    merged, top, total = merge(
                        [(sums[h, dest, :, lanes], *mine[half]), (got[h, step - 1, side, :, lanes], *theirs[half])]
                    )
                    held[h, step - 1, side, :, lanes] = merged.astype(jnp.bfloat16)
                    write_stats(to_stats, half, top, total)
            for copy in sum_copies(h, step, side):
                copy.start()

    def gathered(h, half):
        lanes = pl.ds(half * 128, 128)
        sources = [
            (sums.at[h, at.z], stats.at[h, at.z]),
            (got.at[h, 3, 0], got_stats.at[h, 3, 0]),
            (got.at[h, 3, 1], got_stats.at[h, 3, 1]),
        ]
        return [(ref[:, lanes], *read_stats(stat)[half]) for ref, stat in sources]

    def y_copies(h):
        return [
            remote(y_held.at[h], y_got.at[h], y_send.at[h, 0], y_recv.at[h, 0], at.to_y()),
            remote(y_held_stats.at[h], y_got_stats.at[h], y_send.at[h, 1], y_recv.at[h, 1], at.to_y()),
        ]

    def sum_end(h):
        for side in (0, 1):
            for copy in sum_copies(h, 3, side):
                copy.wait_recv()
        for half in (0, 1):

            @pl.when(at.yh != half)
            def _():
                merged, top, total = merge(gathered(h, half))
                y_held[h] = merged.astype(jnp.bfloat16)
                write_stats(y_held_stats.at[h], 0, top, total)

        for copy in y_copies(h):
            copy.start()

    stretch_out = (at.zh + 3) % 4

    def finish(h):
        for copy in y_copies(h):
            copy.wait_recv()
        r = lax.broadcasted_iota(jnp.int32, (128, HEAD_DIM), 0)
        position = (r // 32) * 256 + at.yh * 128 + ((r // 16) % 2) * 64 + at.zl * 32 + at.core * 16 + r % 16
        keep = position < tok_count[stretch_out]
        cols = pl.ds(h * HEAD_DIM, HEAD_DIM)
        gate_row = gates[pl.ds(noise_levels[stretch_out], 1), :][:, h * HEAD_DIM : (h + 1) * HEAD_DIM]
        for half in (0, 1):

            @pl.when(at.yh == half)
            def _():
                merged, top, total = merge(gathered(h, half) + [(y_got[h], *read_stats(y_got_stats.at[h])[0])])
                attended = merged / total
                mean_sq = jnp.mean(attended * attended, axis=0, keepdims=True)
                normed = (attended * lax.rsqrt(mean_sq + 1e-6)).T
                ready[:, cols] = jnp.where(keep, normed * gate_row, 0.0).astype(jnp.bfloat16)

        dst = out.at[0, :, aligned(at.member * COLS + h * HEAD_DIM, HEAD_DIM)]
        for off in GROUP:
            target, member = at.peer(*off)
            remote(ready.at[aligned(member * ROWS, ROWS), cols], dst, out_send.at[h], out_recv.at[h], target).start()
        pltpu.make_async_copy(ready.at[aligned(at.member * ROWS, ROWS), cols], dst, out_recv.at[h]).start()

    def query_rows(h, dest):
        plane = (dest + 6) % 8
        return plane // 2, queries[plane, :, h * HEAD_DIM : (h + 1) * HEAD_DIM]

    def fold(x, op):
        return op(x.reshape(-1, 8, QUERIES), axis=0)

    def stage(cur, cur_scores, top, nxt, nxt_scores):
        if cur is not None:
            h, dest = cur
            stretch = (dest + 6) % 8 // 2
            shift = top * SCALE
            total8 = jnp.zeros((8, QUERIES), jnp.float32)
            product = None
        if nxt is not None:
            next_h = nxt[0]
            next_stretch, q_head = query_rows(*nxt)
            top8 = jnp.full((8, QUERIES), MASKED, jnp.float32)
        for e in range(PER_SRC):
            rows = slice(e * KEYS, (e + 1) * KEYS)
            if nxt is not None:
                scores = dot_rows(kept[next_h, picked[next_stretch, e]], q_head)
                nxt_scores[rows, :] = scores
                live = e < picked[next_stretch, PER_SRC]
                top8 = jnp.maximum(top8, jnp.where(live, fold(scores, jnp.max), MASKED))
            if cur is not None:
                live = e < picked[stretch, PER_SRC]
                weights = jnp.exp2(cur_scores[rows, :] * SCALE - jnp.where(live, shift, UNUSED))
                total8 = total8 + fold(weights, jnp.sum)
                part = jnp.dot(
                    turned[h, picked[stretch, e]], weights.astype(jnp.bfloat16), preferred_element_type=jnp.float32
                )
                product = part if product is None else product + part
        if cur is not None:
            sums[h, dest] = product.astype(jnp.bfloat16)
            total = jnp.sum(total8, axis=0, keepdims=True)
            for half in (0, 1):
                lanes = slice(half * 128, half * 128 + 128)
                write_stats(stats.at[h, dest], half, shift[:, lanes], total[:, lanes])
        return None if nxt is None else jnp.max(top8, axis=0, keepdims=True)

    def add_own(h, dest):
        @pl.when((dest + 6) % 8 // 2 == at.zh)
        def _():
            _, q_head = query_rows(h, dest)
            bias = own_bias[...]
            scores = dot_rows(kept[h, CLEAN], q_head) + jnp.concatenate([bias, bias], axis=1)
            shift = jnp.max(scores, axis=0, keepdims=True) * SCALE
            weights = jnp.exp2(scores * SCALE - shift)
            total = jnp.sum(weights, axis=0, keepdims=True)
            product = jnp.dot(turned[h, CLEAN], weights.astype(jnp.bfloat16), preferred_element_type=jnp.float32)
            before = read_stats(stats.at[h, dest])
            for half in (0, 1):
                lanes = slice(half * 128, half * 128 + 128)
                merged, top, total_both = merge(
                    [(sums[h, dest, :, lanes], *before[half]), (product[:, lanes], shift[:, lanes], total[:, lanes])]
                )
                sums[h, dest, :, lanes] = merged.astype(jnp.bfloat16)
                write_stats(stats.at[h, dest], half, top, total_both)

    gate_copy = pltpu.make_async_copy(gate_table.at[:, aligned(at.member * COLS, COLS)], gates, gate_sem)

    for copy in staging:
        copy.wait()
    for h in range(LOCAL_HEADS):
        send_keys(h)
    gate_copy.start()
    for stretch in range(STRETCHES):
        count = jnp.int32(0)
        chosen = [jnp.int32(0)] * PER_SRC
        for entry in range(LIST):
            block = block_list[stretch, entry]
            hit = jnp.logical_and(block // CLEAN == at.zh, entry < list_len[stretch])
            for e in range(PER_SRC):
                chosen[e] = jnp.where(jnp.logical_and(hit, count == e), block % CLEAN, chosen[e])
            count = count + jnp.where(hit, 1, 0)
        for e in range(PER_SRC):
            picked[stretch, e] = chosen[e]
        picked[stretch, PER_SRC] = count
    j = lax.broadcasted_iota(jnp.int32, (KEYS, 128), 0)
    position = ((j // 32) % 4) * 256 + at.yh * 128 + ((j // 16) % 2) * 64 + at.zl * 32 + (j // 128) * 16 + j % 16
    own_bias[...] = jnp.where(position < tok_count[at.zh], 0.0, MASKED)
    drain(queries.at[at.z], q_recv)
    for h in range(LOCAL_HEADS):
        ring_step(h, 0)
    share_keys(0)
    for h in range(LOCAL_HEADS):
        ring_step(h, 1)
    take_keys(0)
    for h in range(LOCAL_HEADS):
        ring_step(h, 2)
    share_keys(1)
    gate_copy.wait()
    take_keys(1)

    def dest_at(u):
        away = 4 - (u + 1) // 2
        return jnp.where(u % 2 == 1, at.z + away, at.z + 8 - away) % 8

    def first_heads(u, top):
        pl.when(u == 1)(lambda: ring_step(0, 3))
        pl.when(u == 1)(lambda: ring_step(1, 3))
        pl.when(u == 2)(lambda: ring_step(2, 3))
        pl.when(u == 3)(lambda: ring_end(0))
        pl.when(u == 3)(lambda: ring_end(1))
        pl.when(u == 5)(lambda: share_keys(2))
        dest, later = dest_at(u), dest_at(jnp.minimum(u + 1, 7))
        top = stage((0, dest), scores0, top, (1, dest), scores1)
        add_own(0, dest)
        top = stage((1, dest), scores1, top, (0, later), scores0)
        add_own(1, dest)
        for h in (0, 1):
            pl.when(u == 0)(functools.partial(sum_step, h, 0))
            pl.when(u == 2)(functools.partial(sum_step, h, 1))
            pl.when(u == 5)(functools.partial(sum_step, h, 2))
        return top

    top = stage(None, None, None, (0, dest_at(0)), scores0)
    lax.fori_loop(0, 8, first_heads, top)
    take_keys(2)
    ring_end(2)

    def last_head(i, top):
        even, odd, later = dest_at(2 * i), dest_at(2 * i + 1), dest_at(jnp.minimum(2 * i + 2, 7))
        top = stage((2, even), scores0, top, (2, odd), scores1)
        add_own(2, even)
        pl.when(i == 0)(lambda: sum_step(2, 0))
        top = stage((2, odd), scores1, top, (2, later), scores0)
        add_own(2, odd)
        for h in (0, 1):
            pl.when(i == 0)(functools.partial(sum_step, h, 3))
        return top

    top = stage(None, None, None, (2, dest_at(0)), scores0)
    lax.fori_loop(0, 4, last_head, top)
    sum_step(2, 1)
    sum_end(0)
    sum_end(1)
    sum_step(2, 2)
    finish(0)
    finish(1)
    sum_step(2, 3)
    sum_end(2)
    finish(2)

    drain(queries.at[0, pl.ds(0, 15 * ROWS), :], q_send)
    for h in range(LOCAL_HEADS):
        for part, ref in enumerate((keys[h], values[h])):
            drain(ref.at[:, pl.ds(0, 7 * ROWS), :], kv_send.at[h, part])
            share_copy(h, part).wait_send()
        for side in (0, 1):
            for step in range(4):
                ring_copy(h, step, side).wait_send()
                for copy in sum_copies(h, step, side):
                    copy.wait_send()
        for copy in y_copies(h):
            copy.wait_send()
        drain(ready.at[pl.ds(0, 7 * ROWS), pl.ds(0, HEAD_DIM)], out_send.at[h])
        drain(out.at[0, :, pl.ds(0, MEMBERS * HEAD_DIM)], out_recv.at[h])


def shards(q, sk, sv, ck, cv, block_list, list_len, tok_count, noise_levels, gate_table):
    smem = pl.BlockSpec(memory_space=pltpu.SMEM)
    hbm = pl.BlockSpec(memory_space=pltpu.HBM)
    dma = pltpu.SemaphoreType.DMA
    bf, f32 = jnp.bfloat16, jnp.float32
    heads = LOCAL_HEADS
    return pl.pallas_call(
        kernel,
        out_shape=jax.ShapeDtypeStruct((1, ROWS, MEMBERS * COLS), bf),
        in_specs=[smem] * 4 + [hbm] * 6,
        out_specs=hbm,
        scratch_shapes=[pltpu.VMEM((CLEAN + 1, KEYS, HEAD_DIM), bf)] * 6
        + [
            pltpu.VMEM((heads, CLEAN + 1, KEYS, HEAD_DIM), bf),
            pltpu.VMEM((heads, CLEAN + 1, HEAD_DIM, KEYS), bf),
            pltpu.VMEM((PER_SRC * KEYS, QUERIES), f32),
            pltpu.VMEM((PER_SRC * KEYS, QUERIES), f32),
            pltpu.VMEM((2, CLEAN + 1, ROWS, MEMBERS * COLS), bf),
            dma((4,)),
            pltpu.VMEM((8, QUERIES, COLS), bf),
            pltpu.VMEM((KEYS, 128), f32),
            pltpu.SMEM((STRETCHES, PER_SRC + 1), jnp.int32),
            pltpu.VMEM((heads, 8, HEAD_DIM, QUERIES), bf),
            pltpu.VMEM((heads, 8, 8, 128), f32),
            pltpu.VMEM((heads, 3, 2, HEAD_DIM, QUERIES), bf),
            pltpu.VMEM((heads, 3, 2, 8, 128), f32),
            pltpu.VMEM((heads, 4, 2, HEAD_DIM, QUERIES), bf),
            pltpu.VMEM((heads, 4, 2, 8, 128), f32),
            pltpu.VMEM((heads, HEAD_DIM, 128), bf),
            pltpu.VMEM((heads, 8, 128), f32),
            pltpu.VMEM((heads, HEAD_DIM, 128), bf),
            pltpu.VMEM((heads, 8, 128), f32),
            pltpu.VMEM((48, COLS), f32),
            pltpu.VMEM((128, COLS), bf),
            dma((heads, 2)), dma((heads, 2)), dma((heads, 2)), dma((heads, 2)), dma, dma,
            dma((heads, 4, 2)), dma((heads, 4, 2)), dma((heads, 4, 2)), dma((heads, 4, 2)),
            dma((heads, 4, 2)), dma((heads, 4, 2)), dma((heads, 2)), dma((heads, 2)), dma((heads,)), dma((heads,)), dma,
        ],
        compiler_params=pltpu.CompilerParams(
            collective_id=0, has_side_effects=True, vmem_limit_bytes=58 * 1024 * 1024
        ),
    )(block_list, list_len, tok_count, noise_levels, q, sk, sv, ck, cv, gate_table)


def solution(mesh):
    fine = Mesh(mesh.devices.reshape(4, 4, 2, 2, 2, 2), AXES)
    split = P("zh", ("x", "yh", "yl", "zl", "core"), None)
    return jax.shard_map(
        shards, mesh=fine, in_specs=(split,) * 5 + (P(),) * 5, out_specs=split, check_vma=False
    )
```

```python
import functools
import math

import jax
import jax.numpy as jnp
from jax import lax
from jax.experimental import pallas as pl
from jax.experimental.pallas import tpu as pltpu
from jax.sharding import Mesh
from jax.sharding import PartitionSpec as P

HEAD_DIM = 128
LOCAL_HEADS = 3
COLS = LOCAL_HEADS * HEAD_DIM
PER_SRC = 4
MEMBERS = 8
ROWS = 16
CLEAN = 8
LIST = 16
STRETCHES = 4
KEYS = 256
QUERIES = 256
MASKED = -1e30
UNUSED = 1e30
SCALE = 1.4426950408889634 / math.sqrt(HEAD_DIM)
AXES = ("zh", "x", "yh", "yl", "zl", "core")
GROUP = [(dx, dl) for dx in (2, 1, 3, 0) for dl in (1, 0) if (dx, dl) != (0, 0)]
PLANE = [(dx, dh, dl) for dx in (2, 1, 3, 0) for dh in (1, 0) for dl in (1, 0) if (dx, dh, dl) != (0, 0, 0)]


class Place:
    def __init__(self):
        for name in AXES:
            setattr(self, name, lax.axis_index(name))
        self.z = self.zh * 2 + self.zl
        self.member = self.x * 2 + self.yl

    def peer(self, dx, dl):
        px, pyl = (self.x + dx) % 4, (self.yl + dl) % 2
        return {"x": px, "yl": pyl}, px * 2 + pyl

    def in_plane(self, dx, dh, dl):
        target, member = self.peer(dx, dl)
        return dict(target, yh=(self.yh + dh) % 2), member

    def to_z(self, step):
        other = (self.z + step + 8) % 8
        return {"zh": other // 2, "zl": other % 2}

    def to_y(self):
        return {"yh": 1 - self.yh}

    def to_core(self):
        return {"core": 1 - self.core}


def greet(targets):
    barrier = pltpu.get_barrier_semaphore()
    for target in targets:
        pl.semaphore_signal(barrier, inc=1, device_id=target, device_id_type=pl.DeviceIdType.MESH)
    pl.semaphore_wait(barrier, len(targets))


def remote(src, dst, send, recv, target):
    return pltpu.make_async_remote_copy(
        src_ref=src, dst_ref=dst, send_sem=send, recv_sem=recv, device_id=target, device_id_type=pl.DeviceIdType.MESH
    )


def drain(ref, sem):
    pltpu.make_async_copy(ref, ref, sem).wait()


def aligned(start, size):
    return pl.ds(pl.multiple_of(start, size), size)


def dot_rows(a, b):
    return lax.dot_general(a, b, (((1,), (1,)), ((), ())), preferred_element_type=jnp.float32)


def merge(parts):
    top = functools.reduce(jnp.maximum, [t for _, t, _ in parts])
    factors = [jnp.exp2(t - top) for _, t, _ in parts]
    total = functools.reduce(jnp.add, [f * n for f, (_, _, n) in zip(factors, parts)])
    sums = functools.reduce(jnp.add, [s.astype(jnp.float32) * f for f, (s, _, _) in zip(factors, parts)])
    return sums, top, total


def read_stats(ref):
    tile = ref[...]
    return [(tile[i : i + 1], tile[2 + i : 3 + i]) for i in (0, 1)]


def write_stats(ref, half, top, total):
    ref[half : half + 1, :] = top
    ref[2 + half : 3 + half, :] = total


def kernel(
    block_list_hbm, list_len_hbm, tok_count_hbm, noise_levels_hbm, q, sk, sv, ck, cv, gate_table, out,
    block_list, list_len, tok_count, noise_levels, scalar_sem, keys0, keys1, keys2, values0, values1, values2, kept, turned, scores0, scores1, staged, stage_sem, queries, own_bias, picked,
    sums, stats, y_got, y_got_stats, joined, joined_stats, z_got, z_got_stats, gates, ready,
    kv_send, kv_recv, core_send, core_recv, q_send, q_recv, ring_send, ring_recv,
    y_send, y_recv, z_send, z_recv, out_send, out_recv, gate_sem,
):
    at = Place()
    keys, values = (keys0, keys1, keys2), (values0, values1, values2)
    staging = [
        pltpu.make_async_copy(ck, staged.at[0, pl.ds(0, CLEAN)], stage_sem.at[0]),
        pltpu.make_async_copy(cv, staged.at[1, pl.ds(0, CLEAN)], stage_sem.at[1]),
        pltpu.make_async_copy(sk, staged.at[0, pl.ds(CLEAN, 1)], stage_sem.at[2]),
        pltpu.make_async_copy(sv, staged.at[1, pl.ds(CLEAN, 1)], stage_sem.at[3]),
    ]
    scalars = [
        pltpu.make_async_copy(src, dst, scalar_sem.at[n])
        for n, (src, dst) in enumerate(
            (
                (block_list_hbm, block_list), (list_len_hbm, list_len), (tok_count_hbm, tok_count),
                (noise_levels_hbm, noise_levels),
            )
        )
    ]
    for copy in staging + scalars:
        copy.start()
    greet([at.in_plane(*off)[0] for off in PLANE] + [*[at.to_z(k) for k in (1, -1, 2, -2)], at.to_core()])

    q_rows = aligned(at.yh * 128 + at.member * ROWS, ROWS)
    q_dst = queries.at[at.z, q_rows, :]
    for off in PLANE:
        target, member = at.in_plane(*off)
        remote(q.at[0, :, aligned(member * COLS, COLS)], q_dst, q_send, q_recv, target).start()
    pltpu.make_async_copy(q.at[0, :, aligned(at.member * COLS, COLS)], q_dst, q_recv).start()

    slot = aligned((at.core * MEMBERS + at.member) * ROWS, ROWS)
    my_half = aligned(at.core * 128, 128)

    def send_keys(h):
        for part, ref in enumerate((keys[h], values[h])):
            dst = ref.at[:, slot, :]
            for off in GROUP:
                target, member = at.peer(*off)
                cols = aligned(member * COLS + h * HEAD_DIM, HEAD_DIM)
                remote(staged.at[part, :, :, cols], dst, kv_send.at[h, part], kv_recv.at[h, part], target).start()
            cols = aligned(at.member * COLS + h * HEAD_DIM, HEAD_DIM)
            pltpu.make_async_copy(staged.at[part, :, :, cols], dst, kv_recv.at[h, part]).start()

    def share_copy(h, part):
        ref = (keys[h], values[h])[part].at[:, my_half, :]
        return remote(ref, ref, core_send.at[h, part], core_recv.at[h, part], at.to_core())

    def share_keys(h):
        for part, ref in enumerate((keys[h], values[h])):
            drain(ref.at[:, my_half, :], kv_recv.at[h, part])
            share_copy(h, part).start()

    def take_keys(h):
        for part in (0, 1):
            share_copy(h, part).wait_recv()

        def turn(block, carry):
            kept[h, block] = keys[h][block]
            turned[h, block] = values[h][block].T
            return carry

        lax.fori_loop(0, CLEAN + 1, turn, 0)

    def ring_copy(h, step, side):
        plane = (at.z - step + 8) % 8 if side == 0 else (at.z + step) % 8
        rows = pl.ds(side * 128, 128) if step == 3 else pl.ds(0, QUERIES)
        piece = queries.at[plane, rows, pl.ds(h * HEAD_DIM, HEAD_DIM)]
        return remote(
            piece, piece, ring_send.at[h, step, side], ring_recv.at[h, step, side], at.to_z(1 if side == 0 else -1)
        )

    def ring_step(h, step):
        for side in (0, 1):
            if step > 0:
                ring_copy(h, step - 1, side).wait_recv()
            ring_copy(h, step, side).start()

    def ring_end(h):
        for side in (0, 1):
            ring_copy(h, 3, side).wait_recv()

    my_lanes, other_lanes = aligned(at.yh * 128, 128), aligned((1 - at.yh) * 128, 128)

    def y_copies(h, dest):
        return [
            remote(
                sums.at[h, dest, :, other_lanes], y_got.at[h, dest], y_send.at[h, dest, 0], y_recv.at[h, dest, 0], at.to_y()
            ),
            remote(stats.at[h, dest], y_got_stats.at[h, dest], y_send.at[h, dest, 1], y_recv.at[h, dest, 1], at.to_y()),
        ]

    def send_y(h, dest):
        for copy in y_copies(h, dest):
            copy.start()

    def z_copies(h, dest, slot, step):
        src, target = joined.at[h, dest], at.to_z(step)
        return [
            remote(src, z_got.at[h, slot], z_send.at[h, slot, 0], z_recv.at[h, slot, 0], target),
            remote(
                joined_stats.at[h, dest], z_got_stats.at[h, slot], z_send.at[h, slot, 1], z_recv.at[h, slot, 1], target
            ),
        ]

    def z_start(h, dest, slot, step):
        for copy in z_copies(h, dest, slot, step):
            copy.start()

    def z_part(h, slot):
        drain(z_got.at[h, slot], z_recv.at[h, slot, 0])
        drain(z_got_stats.at[h, slot], z_recv.at[h, slot, 1])
        return (z_got[h, slot], *read_stats(z_got_stats.at[h, slot])[0])

    def own_part(h, dest):
        return (joined[h, dest], *read_stats(joined_stats.at[h, dest])[0])

    def put_joined(h, dest, merged, top, total):
        joined[h, dest] = merged.astype(jnp.bfloat16)
        write_stats(joined_stats.at[h, dest], 0, top, total)

    def middle(h):
        for side in (0, 1):
            dest = (at.z + (6, 2)[side]) % 8

            @pl.when(at.z % 2 == side)
            def _():
                put_joined(h, dest, *merge([own_part(h, dest), z_part(h, 2 + side), z_part(h, 4 + side)]))

            @pl.when(at.z % 2 != side)
            def _():
                put_joined(h, dest, *merge([own_part(h, dest), z_part(h, 2 + side)]))

            z_start(h, dest, 6 + side, (-2, 2)[side])

    def pick_half(ref):
        tile = ref[...]
        return [jnp.where(at.yh == 0, tile[i : i + 1], tile[i + 1 : i + 2]) for i in (0, 2)]

    def join_y(h, dest):
        for copy in y_copies(h, dest):
            copy.wait_recv()
        merged, top, total = merge(
            [
                (sums[h, dest, :, my_lanes], *pick_half(stats.at[h, dest])),
                (y_got[h, dest], *pick_half(y_got_stats.at[h, dest])),
            ]
        )
        put_joined(h, dest, merged, top, total)
        away = (at.z - dest + 8) % 8
        above = away < 4

        @pl.when(away % 2 == 1)
        def _():
            slot = jnp.where(above, 0, 1) + jnp.where(jnp.logical_or(away == 3, away == 5), 2, 0)
            z_start(h, dest, slot, jnp.where(above, -1, 1))

        @pl.when(away == 4)
        def _():
            even = at.z % 2 == 0
            z_start(h, dest, jnp.where(even, 4, 5), jnp.where(even, -2, 2))

    stretch_out = (at.zh + 3) % 4

    def finish(h):
        parts = [own_part(h, at.z)] + [z_part(h, slot) for slot in (0, 1, 6, 7)]
        r = lax.broadcasted_iota(jnp.int32, (128, HEAD_DIM), 0)
        position = (r // 32) * 256 + at.yh * 128 + ((r // 16) % 2) * 64 + at.zl * 32 + at.core * 16 + r % 16
        keep = position < tok_count[stretch_out]
        cols = pl.ds(h * HEAD_DIM, HEAD_DIM)
        gate_row = gates[pl.ds(noise_levels[stretch_out], 1), :][:, h * HEAD_DIM : (h + 1) * HEAD_DIM]
        merged, top, total = merge(parts)
        attended = merged / total
        mean_sq = jnp.mean(attended * attended, axis=0, keepdims=True)
        normed = (attended * lax.rsqrt(mean_sq + 1e-6)).T
        ready[:, cols] = jnp.where(keep, normed * gate_row, 0.0).astype(jnp.bfloat16)

        dst = out.at[0, :, aligned(at.member * COLS + h * HEAD_DIM, HEAD_DIM)]
        for off in GROUP:
            target, member = at.peer(*off)
            remote(ready.at[aligned(member * ROWS, ROWS), cols], dst, out_send.at[h], out_recv.at[h], target).start()
        pltpu.make_async_copy(ready.at[aligned(at.member * ROWS, ROWS), cols], dst, out_recv.at[h]).start()

    def query_rows(h, dest):
        plane = (dest + 6) % 8
        return plane // 2, queries[plane, :, aligned(h * HEAD_DIM, HEAD_DIM)]

    def fold(x, op):
        return op(x.reshape(-1, 8, QUERIES), axis=0)

    def stage(cur, cur_scores, top, nxt, nxt_scores):
        if cur is not None:
            h, dest = cur
            stretch = (dest + 6) % 8 // 2
            shift = top * SCALE
            total8 = jnp.zeros((8, QUERIES), jnp.float32)
            product = None
        if nxt is not None:
            next_h = nxt[0]
            next_stretch, q_head = query_rows(*nxt)
            top8 = jnp.full((8, QUERIES), MASKED, jnp.float32)
        for e in range(PER_SRC):
            rows = slice(e * KEYS, (e + 1) * KEYS)
            if nxt is not None:
                scores = dot_rows(kept[next_h, picked[next_stretch, e]], q_head)
                nxt_scores[rows, :] = scores
                live = e < picked[next_stretch, PER_SRC]
                top8 = jnp.maximum(top8, jnp.where(live, fold(scores, jnp.max), MASKED))
            if cur is not None:
                live = e < picked[stretch, PER_SRC]
                weights = jnp.exp2(cur_scores[rows, :] * SCALE - jnp.where(live, shift, UNUSED))
                total8 = total8 + fold(weights, jnp.sum)
                part = jnp.dot(
                    turned[h, picked[stretch, e]], weights.astype(jnp.bfloat16), preferred_element_type=jnp.float32
                )
                product = part if product is None else product + part
        if cur is not None:
            sums[h, dest] = product.astype(jnp.bfloat16)
            total = jnp.sum(total8, axis=0, keepdims=True)
            for half in (0, 1):
                lanes = slice(half * 128, half * 128 + 128)
                write_stats(stats.at[h, dest], half, shift[:, lanes], total[:, lanes])
        return None if nxt is None else jnp.max(top8, axis=0, keepdims=True)

    def add_own(h, dest):
        @pl.when((dest + 6) % 8 // 2 == at.zh)
        def _():
            _, q_head = query_rows(h, dest)
            bias = own_bias[...]
            scores = dot_rows(kept[h, CLEAN], q_head) + jnp.concatenate([bias, bias], axis=1)
            shift = jnp.max(scores, axis=0, keepdims=True) * SCALE
            weights = jnp.exp2(scores * SCALE - shift)
            total = jnp.sum(weights, axis=0, keepdims=True)
            product = jnp.dot(turned[h, CLEAN], weights.astype(jnp.bfloat16), preferred_element_type=jnp.float32)
            before = read_stats(stats.at[h, dest])
            for half in (0, 1):
                lanes = slice(half * 128, half * 128 + 128)
                merged, top, total_both = merge(
                    [(sums[h, dest, :, lanes], *before[half]), (product[:, lanes], shift[:, lanes], total[:, lanes])]
                )
                sums[h, dest, :, lanes] = merged.astype(jnp.bfloat16)
                write_stats(stats.at[h, dest], half, top, total_both)

    gate_copy = pltpu.make_async_copy(gate_table.at[:, aligned(at.member * COLS, COLS)], gates, gate_sem)

    for copy in staging:
        copy.wait()
    for h in range(LOCAL_HEADS):
        send_keys(h)
    gate_copy.start()
    for copy in scalars:
        copy.wait()
    for stretch in range(STRETCHES):
        count = jnp.int32(0)
        chosen = [jnp.int32(0)] * PER_SRC
        for entry in range(LIST):
            block = block_list[stretch, entry]
            hit = jnp.logical_and(block // CLEAN == at.zh, entry < list_len[stretch])
            for e in range(PER_SRC):
                chosen[e] = jnp.where(jnp.logical_and(hit, count == e), block % CLEAN, chosen[e])
            count = count + jnp.where(hit, 1, 0)
        for e in range(PER_SRC):
            picked[stretch, e] = chosen[e]
        picked[stretch, PER_SRC] = count
    j = lax.broadcasted_iota(jnp.int32, (KEYS, 128), 0)
    position = ((j // 32) % 4) * 256 + at.yh * 128 + ((j // 16) % 2) * 64 + at.zl * 32 + (j // 128) * 16 + j % 16
    own_bias[...] = jnp.where(position < tok_count[at.zh], 0.0, MASKED)
    drain(queries.at[at.z], q_recv)
    for h in range(LOCAL_HEADS):
        ring_step(h, 0)
    for h in range(LOCAL_HEADS):
        ring_step(h, 1)
    share_keys(0)
    gate_copy.wait()
    take_keys(0)

    def unit_at(p):
        near, far = p < 10, p < 16
        h = jnp.where(near, p // 5, jnp.where(far, p % 2, 2))
        u = jnp.where(near, p % 5, jnp.where(far, p // 2, p - 16))
        near_first = 2 + jnp.where(u % 2 == 1, (u + 1) // 2, 8 - u // 2)
        far_first = jnp.where(u % 2 == 1, 3 - u // 2, 4 + u // 2)
        return h, (at.z + jnp.where(far, near_first, far_first)) % 8

    def pair(i, top):
        for h in range(LOCAL_HEADS):
            pl.when(i == 1)(functools.partial(ring_step, h, 2))
        pl.when(i == 2)(lambda: share_keys(1))
        pl.when(i == 2)(lambda: take_keys(1))
        for h in range(LOCAL_HEADS):
            pl.when(i == 3)(functools.partial(ring_step, h, 3))
        for h in (0, 1):
            pl.when(i == 6)(functools.partial(ring_end, h))
        pl.when(i == 6)(lambda: share_keys(2))
        pl.when(i == 7)(lambda: take_keys(2))
        pl.when(i == 7)(lambda: ring_end(2))
        even, odd, later = unit_at(2 * i), unit_at(2 * i + 1), unit_at(jnp.minimum(2 * i + 2, 23))
        top = stage(even, scores0, top, odd, scores1)
        add_own(*even)
        send_y(*even)
        top = stage(odd, scores1, top, later, scores0)
        add_own(*odd)
        send_y(*odd)

        @pl.when(i >= 6)
        def _():
            lax.fori_loop(3 * i - 18, 3 * i - 15, join, 0)

        pl.when(i == 11)(lambda: middle(0))

        return top

    def join(p, carry):
        join_y(*unit_at(p))
        return carry

    lax.fori_loop(0, 12, pair, stage(None, None, None, unit_at(0), scores0))
    middle(1)
    lax.fori_loop(18, 21, join, 0)
    middle(2)
    finish(0)
    lax.fori_loop(21, 24, join, 0)
    finish(1)
    finish(2)

    drain(queries.at[0, pl.ds(0, 15 * ROWS), :], q_send)
    for h in range(LOCAL_HEADS):
        for part, ref in enumerate((keys[h], values[h])):
            drain(ref.at[:, pl.ds(0, 7 * ROWS), :], kv_send.at[h, part])
            share_copy(h, part).wait_send()
        for side in (0, 1):
            for step in range(4):
                ring_copy(h, step, side).wait_send()
        for k in range(8):
            for copy in y_copies(h, (at.z + k) % 8):
                copy.wait_send()
        for slot in (0, 1, 2, 3, 6, 7):
            for copy in z_copies(h, at.z, slot, 1):
                copy.wait_send()
        for copy in z_copies(h, at.z, 4 + at.z % 2, 1):
            copy.wait_send()
        drain(ready.at[pl.ds(0, 7 * ROWS), pl.ds(0, HEAD_DIM)], out_send.at[h])
        drain(out.at[0, :, pl.ds(0, MEMBERS * HEAD_DIM)], out_recv.at[h])


def shards(q, sk, sv, ck, cv, block_list, list_len, tok_count, noise_levels, gate_table):
    hbm = pl.BlockSpec(memory_space=pltpu.HBM)
    dma = pltpu.SemaphoreType.DMA
    bf, f32 = jnp.bfloat16, jnp.float32
    heads = LOCAL_HEADS
    return pl.pallas_call(
        kernel,
        out_shape=jax.ShapeDtypeStruct((1, ROWS, MEMBERS * COLS), bf),
        in_specs=[hbm] * 10,
        out_specs=hbm,
        scratch_shapes=[
            pltpu.SMEM((STRETCHES, LIST), jnp.int32),
            *[pltpu.SMEM((STRETCHES,), jnp.int32)] * 3,
            dma((4,)),
        ]
        + [pltpu.VMEM((CLEAN + 1, KEYS, HEAD_DIM), bf)] * 6
        + [
            pltpu.VMEM((heads, CLEAN + 1, KEYS, HEAD_DIM), bf),
            pltpu.VMEM((heads, CLEAN + 1, HEAD_DIM, KEYS), bf),
            pltpu.VMEM((PER_SRC * KEYS, QUERIES), f32),
            pltpu.VMEM((PER_SRC * KEYS, QUERIES), f32),
            pltpu.VMEM((2, CLEAN + 1, ROWS, MEMBERS * COLS), bf),
            dma((4,)),
            pltpu.VMEM((8, QUERIES, COLS), bf),
            pltpu.VMEM((KEYS, 128), f32),
            pltpu.SMEM((STRETCHES, PER_SRC + 1), jnp.int32),
            pltpu.VMEM((heads, 8, HEAD_DIM, QUERIES), bf),
            pltpu.VMEM((heads, 8, 8, 128), f32),
            pltpu.VMEM((heads, 8, HEAD_DIM, 128), bf),
            pltpu.VMEM((heads, 8, 8, 128), f32),
            pltpu.VMEM((heads, 8, HEAD_DIM, 128), bf),
            pltpu.VMEM((heads, 8, 8, 128), f32),
            pltpu.VMEM((heads, 8, HEAD_DIM, 128), bf),
            pltpu.VMEM((heads, 8, 8, 128), f32),
            pltpu.VMEM((48, COLS), f32),
            pltpu.VMEM((128, COLS), bf),
            dma((heads, 2)), dma((heads, 2)), dma((heads, 2)), dma((heads, 2)), dma, dma,
            dma((heads, 4, 2)), dma((heads, 4, 2)), dma((heads, 8, 2)), dma((heads, 8, 2)),
            dma((heads, 8, 2)), dma((heads, 8, 2)), dma((heads,)), dma((heads,)), dma,
        ],
        compiler_params=pltpu.CompilerParams(
            collective_id=0, has_side_effects=True, vmem_limit_bytes=58 * 1024 * 1024
        ),
    )(block_list, list_len, tok_count, noise_levels, q, sk, sv, ck, cv, gate_table)


def solution(mesh):
    fine = Mesh(mesh.devices.reshape(4, 4, 2, 2, 2, 2), AXES)
    split = P("zh", ("x", "yh", "yl", "zl", "core"), None)
    return jax.shard_map(
        shards, mesh=fine, in_specs=(split,) * 5 + (P(),) * 5, out_specs=split, check_vma=False
    )
```

```python
import functools
import math

import jax
import jax.numpy as jnp
from jax import lax
from jax.experimental import pallas as pl
from jax.experimental.pallas import tpu as pltpu
from jax.sharding import Mesh
from jax.sharding import PartitionSpec as P

HEAD_DIM = 128
LOCAL_HEADS = 3
COLS = LOCAL_HEADS * HEAD_DIM
PER_SRC = 4
MEMBERS = 8
ROWS = 16
CLEAN = 8
LIST = 16
STRETCHES = 4
KEYS = 256
QUERIES = 256
MASKED = -1e30
UNUSED = 1e30
SCALE = 1.4426950408889634 / math.sqrt(HEAD_DIM)
AXES = ("zh", "xh", "xl", "yh", "yl", "zl", "core")
WIDE = 2 * HEAD_DIM
GROUP = [(0, 1), (1, 0), (3, 0), (2, 1), (1, 1), (3, 1), (2, 0)]
PLANE = [(dx, dy) for dx in (2, 1, 3, 0) for dy in (2, 1, 3, 0) if (dx, dy) != (0, 0)]


class Place:
    def __init__(self):
        for name in AXES:
            setattr(self, name, lax.axis_index(name))
        self.x, self.y, self.z = self.xh * 2 + self.xl, self.yh * 2 + self.yl, self.zh * 2 + self.zl
        self.members = (self.x * 2 + self.yl, self.x * 2 + self.yl, self.y * 2 + self.xl)

    def peer(self, h, d, dl):
        if h < 2:
            px, pyl = (self.x + d) % 4, (self.yl + dl) % 2
            return {"xh": px // 2, "xl": px % 2, "yl": pyl}, px * 2 + pyl
        py, pxl = (self.y + d) % 4, (self.xl + dl) % 2
        return {"yh": py // 2, "yl": py % 2, "xl": pxl}, py * 2 + pxl

    def in_plane(self, dx, dy):
        px, py = (self.x + dx) % 4, (self.y + dy) % 4
        target = {"xh": px // 2, "xl": px % 2, "yh": py // 2, "yl": py % 2}
        return target, px * 2 + py % 2, py * 2 + px % 2

    def half(self, h):
        return jnp.where(h == 2, self.xh, self.yh)

    def to_partner(self, h):
        return {"xh": jnp.where(h == 2, 1 - self.xh, self.xh), "yh": jnp.where(h == 2, self.yh, 1 - self.yh)}

    def position(self, h, index, core):
        if h < 2:
            space = ((index // 32) % 4) * 256 + self.yh * 128 + ((index // 16) % 2) * 64
        else:
            space = self.xh * 512 + ((index // 16) % 2) * 256 + ((index // 32) % 4) * 64
        return space + self.zl * 32 + core * 16 + index % 16

    def to_z(self, step):
        other = (self.z + step + 8) % 8
        return {"zh": other // 2, "zl": other % 2}

    def to_core(self):
        return {"core": 1 - self.core}


def greet(targets):
    barrier = pltpu.get_barrier_semaphore()
    for target in targets:
        pl.semaphore_signal(barrier, inc=1, device_id=target, device_id_type=pl.DeviceIdType.MESH)
    pl.semaphore_wait(barrier, len(targets))


def remote(src, dst, send, recv, target):
    return pltpu.make_async_remote_copy(
        src_ref=src, dst_ref=dst, send_sem=send, recv_sem=recv, device_id=target, device_id_type=pl.DeviceIdType.MESH
    )


def drain(ref, sem):
    pltpu.make_async_copy(ref, ref, sem).wait()


def head_columns(h, member):
    return aligned(member * WIDE + h * HEAD_DIM if h < 2 else MEMBERS * WIDE + member * HEAD_DIM, HEAD_DIM)


def aligned(start, size):
    return pl.ds(pl.multiple_of(start, size), size)


def dot_rows(a, b):
    return lax.dot_general(a, b, (((1,), (1,)), ((), ())), preferred_element_type=jnp.float32)


def merge(parts):
    top = functools.reduce(jnp.maximum, [t for _, t, _ in parts])
    factors = [jnp.exp2(t - top) for _, t, _ in parts]
    total = functools.reduce(jnp.add, [f * n for f, (_, _, n) in zip(factors, parts)])
    sums = functools.reduce(jnp.add, [s.astype(jnp.float32) * f for f, (s, _, _) in zip(factors, parts)])
    return sums, top, total


def read_stats(ref):
    tile = ref[...]
    return [(tile[i : i + 1], tile[2 + i : 3 + i]) for i in (0, 1)]


def write_stats(ref, half, top, total):
    ref[half : half + 1, :] = top
    ref[2 + half : 3 + half, :] = total


def kernel(
    block_list_hbm, list_len_hbm, tok_count_hbm, noise_levels_hbm, q, sk, sv, ck, cv, gate_table, out,
    block_list, list_len, tok_count, noise_levels, scalar_sem, keys0, keys1, keys2, values0, values1, values2, kept, turned, scores0, scores1, staged, stage_sem, queries, own_bias, picked,
    sums, stats, y_got, y_got_stats, joined, joined_stats, z_got, z_got_stats, gates, ready,
    kv_send, kv_recv, core_send, core_recv, q_send, q_recv, ring_send, ring_recv,
    y_send, y_recv, z_send, z_recv, out_send, out_recv, gate_sem,
):
    at = Place()
    keys, values = (keys0, keys1, keys2), (values0, values1, values2)
    staging = [
        pltpu.make_async_copy(ck, staged.at[0, pl.ds(0, CLEAN)], stage_sem.at[0]),
        pltpu.make_async_copy(cv, staged.at[1, pl.ds(0, CLEAN)], stage_sem.at[1]),
        pltpu.make_async_copy(sk, staged.at[0, pl.ds(CLEAN, 1)], stage_sem.at[2]),
        pltpu.make_async_copy(sv, staged.at[1, pl.ds(CLEAN, 1)], stage_sem.at[3]),
    ]
    scalars = [
        pltpu.make_async_copy(src, dst, scalar_sem.at[n])
        for n, (src, dst) in enumerate(
            (
                (block_list_hbm, block_list), (list_len_hbm, list_len), (tok_count_hbm, tok_count),
                (noise_levels_hbm, noise_levels),
            )
        )
    ]
    for copy in staging + scalars:
        copy.start()
    greet([at.in_plane(*off)[0] for off in PLANE] + [*[at.to_z(k) for k in (1, -1, 2, -2)], at.to_core()])

    q_dst = [
        queries.at[at.z, aligned(at.yh * 128 + at.members[0] * ROWS, ROWS), pl.ds(0, WIDE)],
        queries.at[at.z, aligned(at.xh * 128 + at.members[2] * ROWS, ROWS), pl.ds(WIDE, HEAD_DIM)],
    ]

    def q_src(member, other):
        return [q.at[0, :, aligned(member * WIDE, WIDE)], q.at[0, :, head_columns(2, other)]]

    for off in PLANE:
        target, member, other = at.in_plane(*off)
        for src, dst in zip(q_src(member, other), q_dst):
            remote(src, dst, q_send, q_recv, target).start()
    for src, dst in zip(q_src(at.members[0], at.members[2]), q_dst):
        pltpu.make_async_copy(src, dst, q_recv).start()

    my_half = aligned(at.core * 128, 128)

    def send_keys(h):
        for part, ref in enumerate((keys[h], values[h])):
            dst = ref.at[:, aligned((at.core * MEMBERS + at.members[h]) * ROWS, ROWS), :]
            for off in GROUP:
                target, member = at.peer(h, *off)
                cols = head_columns(h, member)
                remote(staged.at[part, :, :, cols], dst, kv_send.at[h, part], kv_recv.at[h, part], target).start()
            cols = head_columns(h, at.members[h])
            pltpu.make_async_copy(staged.at[part, :, :, cols], dst, kv_recv.at[h, part]).start()

    def share_copy(h, part):
        ref = (keys[h], values[h])[part].at[:, my_half, :]
        return remote(ref, ref, core_send.at[h, part], core_recv.at[h, part], at.to_core())

    def share_keys(h):
        for part, ref in enumerate((keys[h], values[h])):
            drain(ref.at[:, my_half, :], kv_recv.at[h, part])
            share_copy(h, part).start()

    def take_keys(h):
        for part in (0, 1):
            share_copy(h, part).wait_recv()

        def turn(block, carry):
            kept[h, block] = keys[h][block]
            turned[h, block] = values[h][block].T
            return carry

        lax.fori_loop(0, CLEAN + 1, turn, 0)

    def ring_copy(h, step, side):
        plane = (at.z - step + 8) % 8 if side == 0 else (at.z + step) % 8
        rows = pl.ds(side * 128, 128) if step == 3 else pl.ds(0, QUERIES)
        piece = queries.at[plane, rows, pl.ds(h * HEAD_DIM, HEAD_DIM)]
        return remote(
            piece, piece, ring_send.at[h, step, side], ring_recv.at[h, step, side], at.to_z(1 if side == 0 else -1)
        )

    def ring_step(h, step):
        for side in (0, 1):
            if step > 0:
                ring_copy(h, step - 1, side).wait_recv()
            ring_copy(h, step, side).start()

    def ring_end(h):
        for side in (0, 1):
            ring_copy(h, 3, side).wait_recv()

    def y_copies(h, dest):
        target = at.to_partner(h)
        src = sums.at[h, dest, :, aligned((1 - at.half(h)) * 128, 128)]
        return [
            remote(src, y_got.at[h, dest], y_send.at[h, dest, 0], y_recv.at[h, dest, 0], target),
            remote(stats.at[h, dest], y_got_stats.at[h, dest], y_send.at[h, dest, 1], y_recv.at[h, dest, 1], target),
        ]

    def send_y(h, dest):
        for copy in y_copies(h, dest):
            copy.start()

    def z_copies(h, dest, slot, step):
        src, target = joined.at[h, dest], at.to_z(step)
        return [
            remote(src, z_got.at[h, slot], z_send.at[h, slot, 0], z_recv.at[h, slot, 0], target),
            remote(
                joined_stats.at[h, dest], z_got_stats.at[h, slot], z_send.at[h, slot, 1], z_recv.at[h, slot, 1], target
            ),
        ]

    def z_start(h, dest, slot, step):
        for copy in z_copies(h, dest, slot, step):
            copy.start()

    def z_part(h, slot):
        drain(z_got.at[h, slot], z_recv.at[h, slot, 0])
        drain(z_got_stats.at[h, slot], z_recv.at[h, slot, 1])
        return (z_got[h, slot], *read_stats(z_got_stats.at[h, slot])[0])

    def own_part(h, dest):
        return (joined[h, dest], *read_stats(joined_stats.at[h, dest])[0])

    def put_joined(h, dest, merged, top, total):
        joined[h, dest] = merged.astype(jnp.bfloat16)
        write_stats(joined_stats.at[h, dest], 0, top, total)

    def middle(h):
        for side in (0, 1):
            dest = (at.z + (6, 2)[side]) % 8

            @pl.when(at.z % 2 == side)
            def _():
                put_joined(h, dest, *merge([own_part(h, dest), z_part(h, 2 + side), z_part(h, 4 + side)]))

            @pl.when(at.z % 2 != side)
            def _():
                put_joined(h, dest, *merge([own_part(h, dest), z_part(h, 2 + side)]))

            z_start(h, dest, 6 + side, (-2, 2)[side])

    def pick_half(h, ref):
        tile = ref[...]
        return [jnp.where(at.half(h) == 0, tile[i : i + 1], tile[i + 1 : i + 2]) for i in (0, 2)]

    def join_y(h, dest):
        for copy in y_copies(h, dest):
            copy.wait_recv()
        merged, top, total = merge(
            [
                (sums[h, dest, :, aligned(at.half(h) * 128, 128)], *pick_half(h, stats.at[h, dest])),
                (y_got[h, dest], *pick_half(h, y_got_stats.at[h, dest])),
            ]
        )
        put_joined(h, dest, merged, top, total)
        away = (at.z - dest + 8) % 8
        above = away < 4

        @pl.when(away % 2 == 1)
        def _():
            slot = jnp.where(above, 0, 1) + jnp.where(jnp.logical_or(away == 3, away == 5), 2, 0)
            z_start(h, dest, slot, jnp.where(above, -1, 1))

        @pl.when(away == 4)
        def _():
            even = at.z % 2 == 0
            z_start(h, dest, jnp.where(even, 4, 5), jnp.where(even, -2, 2))

    stretch_out = (at.zh + 3) % 4

    def finish(h):
        parts = [own_part(h, at.z)] + [z_part(h, slot) for slot in (0, 1, 6, 7)]
        r = lax.broadcasted_iota(jnp.int32, (128, HEAD_DIM), 0)
        position = at.position(h, r, at.core)
        keep = position < tok_count[stretch_out]
        cols = pl.ds(h * HEAD_DIM, HEAD_DIM)
        gate_row = gates[pl.ds(noise_levels[stretch_out], 1), :][:, h * HEAD_DIM : (h + 1) * HEAD_DIM]
        merged, top, total = merge(parts)
        attended = merged / total
        mean_sq = jnp.mean(attended * attended, axis=0, keepdims=True)
        normed = (attended * lax.rsqrt(mean_sq + 1e-6)).T
        ready[:, cols] = jnp.where(keep, normed * gate_row, 0.0).astype(jnp.bfloat16)

        dst = out.at[0, :, head_columns(h, at.members[h])]
        for off in GROUP:
            target, member = at.peer(h, *off)
            remote(ready.at[aligned(member * ROWS, ROWS), cols], dst, out_send.at[h], out_recv.at[h], target).start()
        pltpu.make_async_copy(ready.at[aligned(at.members[h] * ROWS, ROWS), cols], dst, out_recv.at[h]).start()

    def query_rows(h, dest):
        plane = (dest + 6) % 8
        return plane // 2, queries[plane, :, aligned(h * HEAD_DIM, HEAD_DIM)]

    def fold(x, op):
        return op(x.reshape(-1, 8, QUERIES), axis=0)

    def stage(cur, cur_scores, top, nxt, nxt_scores):
        if cur is not None:
            h, dest = cur
            stretch = (dest + 6) % 8 // 2
            shift = top * SCALE
            total8 = jnp.zeros((8, QUERIES), jnp.float32)
            product = None
        if nxt is not None:
            next_h = nxt[0]
            next_stretch, q_head = query_rows(*nxt)
            top8 = jnp.full((8, QUERIES), MASKED, jnp.float32)
        for e in range(PER_SRC):
            rows = slice(e * KEYS, (e + 1) * KEYS)
            if nxt is not None:
                scores = dot_rows(kept[next_h, picked[next_stretch, e]], q_head)
                nxt_scores[rows, :] = scores
                live = e < picked[next_stretch, PER_SRC]
                top8 = jnp.maximum(top8, jnp.where(live, fold(scores, jnp.max), MASKED))
            if cur is not None:
                live = e < picked[stretch, PER_SRC]
                weights = jnp.exp2(cur_scores[rows, :] * SCALE - jnp.where(live, shift, UNUSED))
                total8 = total8 + fold(weights, jnp.sum)
                part = jnp.dot(
                    turned[h, picked[stretch, e]], weights.astype(jnp.bfloat16), preferred_element_type=jnp.float32
                )
                product = part if product is None else product + part
        if cur is not None:
            sums[h, dest] = product.astype(jnp.bfloat16)
            total = jnp.sum(total8, axis=0, keepdims=True)
            for half in (0, 1):
                lanes = slice(half * 128, half * 128 + 128)
                write_stats(stats.at[h, dest], half, shift[:, lanes], total[:, lanes])
        return None if nxt is None else jnp.max(top8, axis=0, keepdims=True)

    def add_own(h, dest):
        @pl.when((dest + 6) % 8 // 2 == at.zh)
        def _():
            _, q_head = query_rows(h, dest)
            bias = own_bias[jnp.where(h == 2, 1, 0)]
            scores = dot_rows(kept[h, CLEAN], q_head) + jnp.concatenate([bias, bias], axis=1)
            shift = jnp.max(scores, axis=0, keepdims=True) * SCALE
            weights = jnp.exp2(scores * SCALE - shift)
            total = jnp.sum(weights, axis=0, keepdims=True)
            product = jnp.dot(turned[h, CLEAN], weights.astype(jnp.bfloat16), preferred_element_type=jnp.float32)
            before = read_stats(stats.at[h, dest])
            for half in (0, 1):
                lanes = slice(half * 128, half * 128 + 128)
                merged, top, total_both = merge(
                    [(sums[h, dest, :, lanes], *before[half]), (product[:, lanes], shift[:, lanes], total[:, lanes])]
                )
                sums[h, dest, :, lanes] = merged.astype(jnp.bfloat16)
                write_stats(stats.at[h, dest], half, top, total_both)

    gate_copies = [
        pltpu.make_async_copy(
            gate_table.at[:, aligned(at.members[0] * WIDE, WIDE)], gates.at[:, pl.ds(0, WIDE)], gate_sem.at[0]
        ),
        pltpu.make_async_copy(
            gate_table.at[:, head_columns(2, at.members[2])], gates.at[:, pl.ds(WIDE, HEAD_DIM)], gate_sem.at[1]
        ),
    ]

    for copy in staging:
        copy.wait()
    for h in range(LOCAL_HEADS):
        send_keys(h)
    for copy in gate_copies:
        copy.start()
    for copy in scalars:
        copy.wait()
    for stretch in range(STRETCHES):
        count = jnp.int32(0)
        chosen = [jnp.int32(0)] * PER_SRC
        for entry in range(LIST):
            block = block_list[stretch, entry]
            hit = jnp.logical_and(block // CLEAN == at.zh, entry < list_len[stretch])
            for e in range(PER_SRC):
                chosen[e] = jnp.where(jnp.logical_and(hit, count == e), block % CLEAN, chosen[e])
            count = count + jnp.where(hit, 1, 0)
        for e in range(PER_SRC):
            picked[stretch, e] = chosen[e]
        picked[stretch, PER_SRC] = count
    j = lax.broadcasted_iota(jnp.int32, (KEYS, 128), 0)
    for n, h in enumerate((0, 2)):
        own_bias[n] = jnp.where(at.position(h, j % 128, j // 128) < tok_count[at.zh], 0.0, MASKED)
    drain(queries.at[at.z], q_recv)
    for step in (0, 1):
        for h in (0, 1):
            ring_step(h, step)
    ring_step(2, 0)
    share_keys(0)
    for copy in gate_copies:
        copy.wait()
    take_keys(0)

    def unit_at(p):
        near, far = p < 10, p < 16
        h = jnp.where(near, p // 5, jnp.where(far, p % 2, 2))
        u = jnp.where(near, p % 5, jnp.where(far, p // 2, p - 16))
        near_first = 2 + jnp.where(u % 2 == 1, (u + 1) // 2, 8 - u // 2)
        far_first = jnp.where(u % 2 == 1, 3 - u // 2, 4 + u // 2)
        return h, (at.z + jnp.where(far, near_first, far_first)) % 8

    def pair(i, top):
        for h in (0, 1):
            pl.when(i == 1)(functools.partial(ring_step, h, 2))
        pl.when(i == 2)(lambda: ring_step(2, 1))
        pl.when(i == 2)(lambda: share_keys(1))
        pl.when(i == 2)(lambda: take_keys(1))
        for h in (0, 1):
            pl.when(i == 3)(functools.partial(ring_step, h, 3))
        pl.when(i == 4)(lambda: ring_step(2, 2))
        for h in (0, 1):
            pl.when(i == 6)(functools.partial(ring_end, h))
        pl.when(i == 6)(lambda: ring_step(2, 3))
        pl.when(i == 6)(lambda: share_keys(2))
        pl.when(i == 7)(lambda: take_keys(2))
        pl.when(i == 9)(lambda: ring_end(2))
        even, odd, later = unit_at(2 * i), unit_at(2 * i + 1), unit_at(jnp.minimum(2 * i + 2, 23))
        top = stage(even, scores0, top, odd, scores1)
        add_own(*even)
        send_y(*even)
        top = stage(odd, scores1, top, later, scores0)
        add_own(*odd)
        send_y(*odd)

        @pl.when(i >= 6)
        def _():
            lax.fori_loop(3 * i - 18, 3 * i - 15, join, 0)

        pl.when(i == 11)(lambda: middle(0))

        return top

    def join(p, carry):
        join_y(*unit_at(p))
        return carry

    lax.fori_loop(0, 12, pair, stage(None, None, None, unit_at(0), scores0))
    middle(1)
    lax.fori_loop(18, 21, join, 0)
    middle(2)
    finish(0)
    lax.fori_loop(21, 24, join, 0)
    finish(1)
    finish(2)

    drain(queries.at[0, pl.ds(0, 15 * ROWS), :], q_send)
    for h in range(LOCAL_HEADS):
        for part, ref in enumerate((keys[h], values[h])):
            drain(ref.at[:, pl.ds(0, 7 * ROWS), :], kv_send.at[h, part])
            share_copy(h, part).wait_send()
        for side in (0, 1):
            for step in range(4):
                ring_copy(h, step, side).wait_send()
        for k in range(8):
            for copy in y_copies(h, (at.z + k) % 8):
                copy.wait_send()
        for slot in (0, 1, 2, 3, 6, 7):
            for copy in z_copies(h, at.z, slot, 1):
                copy.wait_send()
        for copy in z_copies(h, at.z, 4 + at.z % 2, 1):
            copy.wait_send()
        drain(ready.at[pl.ds(0, 7 * ROWS), pl.ds(0, HEAD_DIM)], out_send.at[h])
        drain(out.at[0, :, pl.ds(0, MEMBERS * HEAD_DIM)], out_recv.at[h])


def shards(q, sk, sv, ck, cv, block_list, list_len, tok_count, noise_levels, gate_table):
    hbm = pl.BlockSpec(memory_space=pltpu.HBM)
    dma = pltpu.SemaphoreType.DMA
    bf, f32 = jnp.bfloat16, jnp.float32
    heads = LOCAL_HEADS
    return pl.pallas_call(
        kernel,
        out_shape=jax.ShapeDtypeStruct((1, ROWS, MEMBERS * COLS), bf),
        in_specs=[hbm] * 10,
        out_specs=hbm,
        scratch_shapes=[
            pltpu.SMEM((STRETCHES, LIST), jnp.int32),
            *[pltpu.SMEM((STRETCHES,), jnp.int32)] * 3,
            dma((4,)),
        ]
        + [pltpu.VMEM((CLEAN + 1, KEYS, HEAD_DIM), bf)] * 6
        + [
            pltpu.VMEM((heads, CLEAN + 1, KEYS, HEAD_DIM), bf),
            pltpu.VMEM((heads, CLEAN + 1, HEAD_DIM, KEYS), bf),
            pltpu.VMEM((PER_SRC * KEYS, QUERIES), f32),
            pltpu.VMEM((PER_SRC * KEYS, QUERIES), f32),
            pltpu.VMEM((2, CLEAN + 1, ROWS, MEMBERS * COLS), bf),
            dma((4,)),
            pltpu.VMEM((8, QUERIES, COLS), bf),
            pltpu.VMEM((2, KEYS, 128), f32),
            pltpu.SMEM((STRETCHES, PER_SRC + 1), jnp.int32),
            pltpu.VMEM((heads, 8, HEAD_DIM, QUERIES), bf),
            pltpu.VMEM((heads, 8, 8, 128), f32),
            pltpu.VMEM((heads, 8, HEAD_DIM, 128), bf),
            pltpu.VMEM((heads, 8, 8, 128), f32),
            pltpu.VMEM((heads, 8, HEAD_DIM, 128), bf),
            pltpu.VMEM((heads, 8, 8, 128), f32),
            pltpu.VMEM((heads, 8, HEAD_DIM, 128), bf),
            pltpu.VMEM((heads, 8, 8, 128), f32),
            pltpu.VMEM((48, COLS), f32),
            pltpu.VMEM((128, COLS), bf),
            dma((heads, 2)), dma((heads, 2)), dma((heads, 2)), dma((heads, 2)), dma, dma,
            dma((heads, 4, 2)), dma((heads, 4, 2)), dma((heads, 8, 2)), dma((heads, 8, 2)),
            dma((heads, 8, 2)), dma((heads, 8, 2)), dma((heads,)), dma((heads,)), dma((2,)),
        ],
        compiler_params=pltpu.CompilerParams(
            collective_id=0, has_side_effects=True, vmem_limit_bytes=58 * 1024 * 1024
        ),
    )(block_list, list_len, tok_count, noise_levels, q, sk, sv, ck, cv, gate_table)


def solution(mesh):
    fine = Mesh(mesh.devices.reshape(4, 2, 2, 2, 2, 2, 2), AXES)
    split = P("zh", ("xh", "xl", "yh", "yl", "zl", "core"), None)
    return jax.shard_map(
        shards, mesh=fine, in_specs=(split,) * 5 + (P(),) * 5, out_specs=split, check_vma=False
    )
```

```python
import functools
import math

import jax
import jax.numpy as jnp
from jax import lax
from jax.experimental import pallas as pl
from jax.experimental.pallas import tpu as pltpu
from jax.sharding import Mesh
from jax.sharding import PartitionSpec as P

HEAD_DIM = 128
LOCAL_HEADS = 3
COLS = LOCAL_HEADS * HEAD_DIM
PER_SRC = 4
MEMBERS = 8
ROWS = 16
CLEAN = 8
LIST = 16
STRETCHES = 4
KEYS = 256
QUERIES = 256
MASKED = -1e30
UNUSED = 1e30
SCALE = 1.4426950408889634 / math.sqrt(HEAD_DIM)
AXES = ("zh", "xh", "xl", "yh", "yl", "zl", "core")
WIDE = 2 * HEAD_DIM
GROUP = [(0, 1), (1, 0), (3, 0), (2, 1), (1, 1), (3, 1), (2, 0)]
PLANE = [(dx, dy) for dx in (2, 1, 3, 0) for dy in (2, 1, 3, 0) if (dx, dy) != (0, 0)]


class Place:
    def __init__(self):
        for name in AXES:
            setattr(self, name, lax.axis_index(name))
        self.x, self.y, self.z = self.xh * 2 + self.xl, self.yh * 2 + self.yl, self.zh * 2 + self.zl
        self.members = (self.x * 2 + self.yl, self.x * 2 + self.yl, self.y * 2 + self.xl)

    def peer(self, h, d, dl):
        if h < 2:
            px, pyl = (self.x + d) % 4, (self.yl + dl) % 2
            return {"xh": px // 2, "xl": px % 2, "yl": pyl}, px * 2 + pyl
        py, pxl = (self.y + d) % 4, (self.xl + dl) % 2
        return {"yh": py // 2, "yl": py % 2, "xl": pxl}, py * 2 + pxl

    def in_plane(self, dx, dy):
        px, py = (self.x + dx) % 4, (self.y + dy) % 4
        target = {"xh": px // 2, "xl": px % 2, "yh": py // 2, "yl": py % 2}
        return target, px * 2 + py % 2, py * 2 + px % 2

    def half(self, h):
        return jnp.where(h == 2, self.xh, self.yh)

    def to_partner(self, h):
        return {"xh": jnp.where(h == 2, 1 - self.xh, self.xh), "yh": jnp.where(h == 2, self.yh, 1 - self.yh)}

    def position(self, h, index, core):
        if h < 2:
            space = ((index // 32) % 4) * 256 + self.yh * 128 + ((index // 16) % 2) * 64
        else:
            space = self.xh * 512 + ((index // 16) % 2) * 256 + ((index // 32) % 4) * 64
        return space + self.zl * 32 + core * 16 + index % 16

    def to_z(self, step):
        other = (self.z + step + 8) % 8
        return {"zh": other // 2, "zl": other % 2}

    def to_core(self):
        return {"core": 1 - self.core}


def greet(targets):
    barrier = pltpu.get_barrier_semaphore()
    for target in targets:
        pl.semaphore_signal(barrier, inc=1, device_id=target, device_id_type=pl.DeviceIdType.MESH)
    pl.semaphore_wait(barrier, len(targets))


def remote(src, dst, send, recv, target):
    return pltpu.make_async_remote_copy(
        src_ref=src, dst_ref=dst, send_sem=send, recv_sem=recv, device_id=target, device_id_type=pl.DeviceIdType.MESH
    )


def drain(ref, sem):
    pltpu.make_async_copy(ref, ref, sem).wait()


def head_columns(h, member):
    return aligned(member * WIDE + h * HEAD_DIM if h < 2 else MEMBERS * WIDE + member * HEAD_DIM, HEAD_DIM)


def aligned(start, size):
    return pl.ds(pl.multiple_of(start, size), size)


def dot_rows(a, b):
    return lax.dot_general(a, b, (((1,), (1,)), ((), ())), preferred_element_type=jnp.float32)


def merge(parts):
    top = functools.reduce(jnp.maximum, [t for _, t, _ in parts])
    factors = [jnp.exp2(t - top) for _, t, _ in parts]
    total = functools.reduce(jnp.add, [f * n for f, (_, _, n) in zip(factors, parts)])
    sums = functools.reduce(jnp.add, [s.astype(jnp.float32) * f for f, (s, _, _) in zip(factors, parts)])
    return sums, top, total


def read_stats(ref):
    tile = ref[...]
    return [(tile[i : i + 1], tile[2 + i : 3 + i]) for i in (0, 1)]


def write_stats(ref, half, top, total):
    ref[half : half + 1, :] = top
    ref[2 + half : 3 + half, :] = total


def kernel(
    block_list_hbm, list_len_hbm, tok_count_hbm, noise_levels_hbm, q, sk, sv, ck, cv, gate_table, out,
    block_list, list_len, tok_count, noise_levels, scalar_sem, keys0, keys1, keys2, values0, values1, values2, kept, turned, scores0, scores1, staged, stage_sem, queries, own_bias, picked,
    sums, stats, y_got, y_got_stats, joined, joined_stats, z_got, z_got_stats, gates, ready,
    kv_send, kv_recv, core_send, core_recv, q_send, q_recv, ring_send, ring_recv,
    y_send, y_recv, z_send, z_recv, out_send, out_recv, gate_sem,
):
    at = Place()
    keys, values = (keys0, keys1, keys2), (values0, values1, values2)
    staging = [
        pltpu.make_async_copy(ck, staged.at[0, pl.ds(0, CLEAN)], stage_sem.at[0]),
        pltpu.make_async_copy(cv, staged.at[1, pl.ds(0, CLEAN)], stage_sem.at[1]),
        pltpu.make_async_copy(sk, staged.at[0, pl.ds(CLEAN, 1)], stage_sem.at[2]),
        pltpu.make_async_copy(sv, staged.at[1, pl.ds(CLEAN, 1)], stage_sem.at[3]),
    ]
    scalars = [
        pltpu.make_async_copy(src, dst, scalar_sem.at[n])
        for n, (src, dst) in enumerate(
            (
                (block_list_hbm, block_list), (list_len_hbm, list_len), (tok_count_hbm, tok_count),
                (noise_levels_hbm, noise_levels),
            )
        )
    ]
    for copy in staging + scalars:
        copy.start()
    greet([at.in_plane(*off)[0] for off in PLANE] + [*[at.to_z(k) for k in (1, -1, 2, -2)], at.to_core()])

    q_dst = [
        queries.at[at.z, aligned(at.yh * 128 + at.members[0] * ROWS, ROWS), pl.ds(0, WIDE)],
        queries.at[at.z, aligned(at.xh * 128 + at.members[2] * ROWS, ROWS), pl.ds(WIDE, HEAD_DIM)],
    ]

    def q_src(member, other):
        return [q.at[0, :, aligned(member * WIDE, WIDE)], q.at[0, :, head_columns(2, other)]]

    for off in PLANE:
        target, member, other = at.in_plane(*off)
        for src, dst in zip(q_src(member, other), q_dst):
            remote(src, dst, q_send, q_recv, target).start()
    for src, dst in zip(q_src(at.members[0], at.members[2]), q_dst):
        pltpu.make_async_copy(src, dst, q_recv).start()

    my_half = aligned(at.core * 128, 128)

    def send_keys(h):
        for part, ref in enumerate((keys[h], values[h])):
            dst = ref.at[:, aligned((at.core * MEMBERS + at.members[h]) * ROWS, ROWS), :]
            for off in GROUP:
                target, member = at.peer(h, *off)
                cols = head_columns(h, member)
                remote(staged.at[part, :, :, cols], dst, kv_send.at[h, part], kv_recv.at[h, part], target).start()
            cols = head_columns(h, at.members[h])
            pltpu.make_async_copy(staged.at[part, :, :, cols], dst, kv_recv.at[h, part]).start()

    def share_copy(h, part):
        ref = (keys[h], values[h])[part].at[:, my_half, :]
        return remote(ref, ref, core_send.at[h, part], core_recv.at[h, part], at.to_core())

    def share_keys(h):
        for part, ref in enumerate((keys[h], values[h])):
            drain(ref.at[:, my_half, :], kv_recv.at[h, part])
            share_copy(h, part).start()

    def take_keys(h):
        for part in (0, 1):
            share_copy(h, part).wait_recv()

        def turn(block, carry):
            kept[h, block] = keys[h][block]
            turned[h, block] = values[h][block].T
            return carry

        lax.fori_loop(0, CLEAN + 1, turn, 0)

    def ring_copy(h, step, side):
        plane = (at.z - step + 8) % 8 if side == 0 else (at.z + step) % 8
        rows = pl.ds(side * 128, 128) if step == 3 else pl.ds(0, QUERIES)
        piece = queries.at[plane, rows, pl.ds(h * HEAD_DIM, HEAD_DIM)]
        return remote(
            piece, piece, ring_send.at[h, step, side], ring_recv.at[h, step, side], at.to_z(1 if side == 0 else -1)
        )

    def ring_step(h, step):
        for side in (0, 1):
            if step > 0:
                ring_copy(h, step - 1, side).wait_recv()
            ring_copy(h, step, side).start()

    def ring_end(h):
        for side in (0, 1):
            ring_copy(h, 3, side).wait_recv()

    def y_copies(h, dest):
        target = at.to_partner(h)
        src = sums.at[h, dest, :, aligned((1 - at.half(h)) * 128, 128)]
        return [
            remote(src, y_got.at[h, dest], y_send.at[h, dest, 0], y_recv.at[h, dest, 0], target),
            remote(stats.at[h, dest], y_got_stats.at[h, dest], y_send.at[h, dest, 1], y_recv.at[h, dest, 1], target),
        ]

    def send_y(h, dest):
        for copy in y_copies(h, dest):
            copy.start()

    def z_copies(h, dest, slot, step):
        src, target = joined.at[h, dest], at.to_z(step)
        return [
            remote(src, z_got.at[h, slot], z_send.at[h, slot, 0], z_recv.at[h, slot, 0], target),
            remote(
                joined_stats.at[h, dest], z_got_stats.at[h, slot], z_send.at[h, slot, 1], z_recv.at[h, slot, 1], target
            ),
        ]

    def z_start(h, dest, slot, step):
        for copy in z_copies(h, dest, slot, step):
            copy.start()

    def z_part(h, slot):
        drain(z_got.at[h, slot], z_recv.at[h, slot, 0])
        drain(z_got_stats.at[h, slot], z_recv.at[h, slot, 1])
        return (z_got[h, slot], *read_stats(z_got_stats.at[h, slot])[0])

    def own_part(h, dest):
        return (joined[h, dest], *read_stats(joined_stats.at[h, dest])[0])

    def put_joined(h, dest, merged, top, total):
        joined[h, dest] = merged.astype(jnp.bfloat16)
        write_stats(joined_stats.at[h, dest], 0, top, total)

    def middle(h):
        for side in (0, 1):
            dest = (at.z + (6, 2)[side]) % 8

            @pl.when(at.z % 2 == side)
            def _():
                put_joined(h, dest, *merge([own_part(h, dest), z_part(h, 2 + side), z_part(h, 4 + side)]))

            @pl.when(at.z % 2 != side)
            def _():
                put_joined(h, dest, *merge([own_part(h, dest), z_part(h, 2 + side)]))

            z_start(h, dest, 6 + side, (-2, 2)[side])

    def pick_half(h, ref):
        tile = ref[...]
        return [jnp.where(at.half(h) == 0, tile[i : i + 1], tile[i + 1 : i + 2]) for i in (0, 2)]

    def join_y(h, dest):
        for copy in y_copies(h, dest):
            copy.wait_recv()
        merged, top, total = merge(
            [
                (sums[h, dest, :, aligned(at.half(h) * 128, 128)], *pick_half(h, stats.at[h, dest])),
                (y_got[h, dest], *pick_half(h, y_got_stats.at[h, dest])),
            ]
        )
        put_joined(h, dest, merged, top, total)
        away = (at.z - dest + 8) % 8
        above = away < 4

        @pl.when(away % 2 == 1)
        def _():
            slot = jnp.where(above, 0, 1) + jnp.where(jnp.logical_or(away == 3, away == 5), 2, 0)
            z_start(h, dest, slot, jnp.where(above, -1, 1))

        @pl.when(away == 4)
        def _():
            even = at.z % 2 == 0
            z_start(h, dest, jnp.where(even, 4, 5), jnp.where(even, -2, 2))

    stretch_out = (at.zh + 3) % 4

    def finish(h):
        parts = [own_part(h, at.z)] + [z_part(h, slot) for slot in (0, 1, 6, 7)]
        r = lax.broadcasted_iota(jnp.int32, (128, HEAD_DIM), 0)
        position = at.position(h, r, at.core)
        keep = position < tok_count[stretch_out]
        cols = pl.ds(h * HEAD_DIM, HEAD_DIM)
        gate_row = gates[pl.ds(noise_levels[stretch_out], 1), :][:, h * HEAD_DIM : (h + 1) * HEAD_DIM]
        merged, top, total = merge(parts)
        attended = merged / total
        mean_sq = jnp.mean(attended * attended, axis=0, keepdims=True)
        normed = (attended * lax.rsqrt(mean_sq + 1e-6)).T
        ready[:, cols] = jnp.where(keep, normed * gate_row, 0.0).astype(jnp.bfloat16)

        dst = out.at[0, :, head_columns(h, at.members[h])]
        for off in GROUP:
            target, member = at.peer(h, *off)
            remote(ready.at[aligned(member * ROWS, ROWS), cols], dst, out_send.at[h], out_recv.at[h], target).start()
        pltpu.make_async_copy(ready.at[aligned(at.members[h] * ROWS, ROWS), cols], dst, out_recv.at[h]).start()

    def query_rows(h, dest):
        plane = (dest + 6) % 8
        return plane // 2, queries[plane, :, aligned(h * HEAD_DIM, HEAD_DIM)]

    def fold(x, op):
        return op(x.reshape(-1, 8, QUERIES), axis=0)

    def stage(cur, cur_scores, top, nxt, nxt_scores):
        if cur is not None:
            h, dest = cur
            stretch = (dest + 6) % 8 // 2
            shift = top * SCALE
            total8 = jnp.zeros((8, QUERIES), jnp.float32)
            product = None
        if nxt is not None:
            next_h = nxt[0]
            next_stretch, q_head = query_rows(*nxt)
            top8 = jnp.full((8, QUERIES), MASKED, jnp.float32)
        for e in range(PER_SRC):
            rows = slice(e * KEYS, (e + 1) * KEYS)
            if nxt is not None:
                scores = dot_rows(kept[next_h, picked[next_stretch, e]], q_head)
                nxt_scores[rows, :] = scores
                live = e < picked[next_stretch, PER_SRC]
                top8 = jnp.maximum(top8, jnp.where(live, fold(scores, jnp.max), MASKED))
            if cur is not None:
                live = e < picked[stretch, PER_SRC]
                weights = jnp.exp2(cur_scores[rows, :] * SCALE - jnp.where(live, shift, UNUSED))
                total8 = total8 + fold(weights, jnp.sum)
                part = jnp.dot(
                    turned[h, picked[stretch, e]], weights.astype(jnp.bfloat16), preferred_element_type=jnp.float32
                )
                product = part if product is None else product + part
        if cur is not None:
            sums[h, dest] = product.astype(jnp.bfloat16)
            total = jnp.sum(total8, axis=0, keepdims=True)
            for half in (0, 1):
                lanes = slice(half * 128, half * 128 + 128)
                write_stats(stats.at[h, dest], half, shift[:, lanes], total[:, lanes])
        return None if nxt is None else jnp.max(top8, axis=0, keepdims=True)

    def add_own(h, dest):
        @pl.when((dest + 6) % 8 // 2 == at.zh)
        def _():
            _, q_head = query_rows(h, dest)
            bias = own_bias[jnp.where(h == 2, 1, 0)]
            scores = dot_rows(kept[h, CLEAN], q_head) + jnp.concatenate([bias, bias], axis=1)
            top = jnp.max(scores, axis=0, keepdims=True)
            shift = top * SCALE
            weights = jnp.exp2(scores * SCALE - jnp.where(top > 0.5 * MASKED, shift, UNUSED))
            total = jnp.sum(weights, axis=0, keepdims=True)
            product = jnp.dot(turned[h, CLEAN], weights.astype(jnp.bfloat16), preferred_element_type=jnp.float32)
            before = read_stats(stats.at[h, dest])
            for half in (0, 1):
                lanes = slice(half * 128, half * 128 + 128)
                merged, top, total_both = merge(
                    [(sums[h, dest, :, lanes], *before[half]), (product[:, lanes], shift[:, lanes], total[:, lanes])]
                )
                sums[h, dest, :, lanes] = merged.astype(jnp.bfloat16)
                write_stats(stats.at[h, dest], half, top, total_both)

    gate_copies = [
        pltpu.make_async_copy(
            gate_table.at[:, aligned(at.members[0] * WIDE, WIDE)], gates.at[:, pl.ds(0, WIDE)], gate_sem.at[0]
        ),
        pltpu.make_async_copy(
            gate_table.at[:, head_columns(2, at.members[2])], gates.at[:, pl.ds(WIDE, HEAD_DIM)], gate_sem.at[1]
        ),
    ]

    for copy in staging:
        copy.wait()
    for h in range(LOCAL_HEADS):
        send_keys(h)
    for copy in gate_copies:
        copy.start()
    for copy in scalars:
        copy.wait()
    for stretch in range(STRETCHES):
        count = jnp.int32(0)
        chosen = [jnp.int32(0)] * PER_SRC
        for entry in range(LIST):
            block = block_list[stretch, entry]
            hit = jnp.logical_and(block // CLEAN == at.zh, entry < list_len[stretch])
            for e in range(PER_SRC):
                chosen[e] = jnp.where(jnp.logical_and(hit, count == e), block % CLEAN, chosen[e])
            count = count + jnp.where(hit, 1, 0)
        for e in range(PER_SRC):
            picked[stretch, e] = chosen[e]
        picked[stretch, PER_SRC] = count
    j = lax.broadcasted_iota(jnp.int32, (KEYS, 128), 0)
    for n, h in enumerate((0, 2)):
        own_bias[n] = jnp.where(at.position(h, j % 128, j // 128) < tok_count[at.zh], 0.0, MASKED)
    drain(queries.at[at.z], q_recv)
    for step in (0, 1):
        for h in (0, 1):
            ring_step(h, step)
    ring_step(2, 0)
    share_keys(0)
    for copy in gate_copies:
        copy.wait()
    take_keys(0)

    def unit_at(p):
        near, far = p < 10, p < 16
        h = jnp.where(near, p // 5, jnp.where(far, p % 2, 2))
        u = jnp.where(near, p % 5, jnp.where(far, p // 2, p - 16))
        near_first = 2 + jnp.where(u % 2 == 1, (u + 1) // 2, 8 - u // 2)
        far_first = jnp.where(u % 2 == 1, 3 - u // 2, 4 + u // 2)
        return h, (at.z + jnp.where(far, near_first, far_first)) % 8

    def pair(i, top):
        for h in (0, 1):
            pl.when(i == 1)(functools.partial(ring_step, h, 2))
        pl.when(i == 2)(lambda: ring_step(2, 1))
        pl.when(i == 2)(lambda: share_keys(1))
        pl.when(i == 2)(lambda: take_keys(1))
        for h in (0, 1):
            pl.when(i == 3)(functools.partial(ring_step, h, 3))
        pl.when(i == 4)(lambda: ring_step(2, 2))
        for h in (0, 1):
            pl.when(i == 6)(functools.partial(ring_end, h))
        pl.when(i == 6)(lambda: ring_step(2, 3))
        pl.when(i == 6)(lambda: share_keys(2))
        pl.when(i == 7)(lambda: take_keys(2))
        pl.when(i == 9)(lambda: ring_end(2))
        even, odd, later = unit_at(2 * i), unit_at(2 * i + 1), unit_at(jnp.minimum(2 * i + 2, 23))
        top = stage(even, scores0, top, odd, scores1)
        add_own(*even)
        send_y(*even)
        top = stage(odd, scores1, top, later, scores0)
        add_own(*odd)
        send_y(*odd)

        @pl.when(i >= 6)
        def _():
            lax.fori_loop(3 * i - 18, 3 * i - 15, join, 0)

        pl.when(i == 11)(lambda: middle(0))

        return top

    def join(p, carry):
        join_y(*unit_at(p))
        return carry

    lax.fori_loop(0, 12, pair, stage(None, None, None, unit_at(0), scores0))
    middle(1)
    lax.fori_loop(18, 21, join, 0)
    middle(2)
    finish(0)
    lax.fori_loop(21, 24, join, 0)
    finish(1)
    finish(2)

    drain(queries.at[0, pl.ds(0, 15 * ROWS), :], q_send)
    for h in range(LOCAL_HEADS):
        for part, ref in enumerate((keys[h], values[h])):
            drain(ref.at[:, pl.ds(0, 7 * ROWS), :], kv_send.at[h, part])
            share_copy(h, part).wait_send()
        for side in (0, 1):
            for step in range(4):
                ring_copy(h, step, side).wait_send()
        for k in range(8):
            for copy in y_copies(h, (at.z + k) % 8):
                copy.wait_send()
        for slot in (0, 1, 2, 3, 6, 7):
            for copy in z_copies(h, at.z, slot, 1):
                copy.wait_send()
        for copy in z_copies(h, at.z, 4 + at.z % 2, 1):
            copy.wait_send()
        drain(ready.at[pl.ds(0, 7 * ROWS), pl.ds(0, HEAD_DIM)], out_send.at[h])
        drain(out.at[0, :, pl.ds(0, MEMBERS * HEAD_DIM)], out_recv.at[h])


def shards(q, sk, sv, ck, cv, block_list, list_len, tok_count, noise_levels, gate_table):
    hbm = pl.BlockSpec(memory_space=pltpu.HBM)
    dma = pltpu.SemaphoreType.DMA
    bf, f32 = jnp.bfloat16, jnp.float32
    heads = LOCAL_HEADS
    return pl.pallas_call(
        kernel,
        out_shape=jax.ShapeDtypeStruct((1, ROWS, MEMBERS * COLS), bf),
        in_specs=[hbm] * 10,
        out_specs=hbm,
        scratch_shapes=[
            pltpu.SMEM((STRETCHES, LIST), jnp.int32),
            *[pltpu.SMEM((STRETCHES,), jnp.int32)] * 3,
            dma((4,)),
        ]
        + [pltpu.VMEM((CLEAN + 1, KEYS, HEAD_DIM), bf)] * 6
        + [
            pltpu.VMEM((heads, CLEAN + 1, KEYS, HEAD_DIM), bf),
            pltpu.VMEM((heads, CLEAN + 1, HEAD_DIM, KEYS), bf),
            pltpu.VMEM((PER_SRC * KEYS, QUERIES), f32),
            pltpu.VMEM((PER_SRC * KEYS, QUERIES), f32),
            pltpu.VMEM((2, CLEAN + 1, ROWS, MEMBERS * COLS), bf),
            dma((4,)),
            pltpu.VMEM((8, QUERIES, COLS), bf),
            pltpu.VMEM((2, KEYS, 128), f32),
            pltpu.SMEM((STRETCHES, PER_SRC + 1), jnp.int32),
            pltpu.VMEM((heads, 8, HEAD_DIM, QUERIES), bf),
            pltpu.VMEM((heads, 8, 8, 128), f32),
            pltpu.VMEM((heads, 8, HEAD_DIM, 128), bf),
            pltpu.VMEM((heads, 8, 8, 128), f32),
            pltpu.VMEM((heads, 8, HEAD_DIM, 128), bf),
            pltpu.VMEM((heads, 8, 8, 128), f32),
            pltpu.VMEM((heads, 8, HEAD_DIM, 128), bf),
            pltpu.VMEM((heads, 8, 8, 128), f32),
            pltpu.VMEM((48, COLS), f32),
            pltpu.VMEM((128, COLS), bf),
            dma((heads, 2)), dma((heads, 2)), dma((heads, 2)), dma((heads, 2)), dma, dma,
            dma((heads, 4, 2)), dma((heads, 4, 2)), dma((heads, 8, 2)), dma((heads, 8, 2)),
            dma((heads, 8, 2)), dma((heads, 8, 2)), dma((heads,)), dma((heads,)), dma((2,)),
        ],
        compiler_params=pltpu.CompilerParams(
            collective_id=0, has_side_effects=True, vmem_limit_bytes=58 * 1024 * 1024
        ),
    )(block_list, list_len, tok_count, noise_levels, q, sk, sv, ck, cv, gate_table)


def solution(mesh):
    fine = Mesh(mesh.devices.reshape(4, 2, 2, 2, 2, 2, 2), AXES)
    split = P("zh", ("xh", "xl", "yh", "yl", "zl", "core"), None)
    return jax.shard_map(
        shards, mesh=fine, in_specs=(split,) * 5 + (P(),) * 5, out_specs=split, check_vma=False
    )
```

```python
import functools
import math

import jax
import jax.numpy as jnp
from jax import lax
from jax.experimental import pallas as pl
from jax.experimental.pallas import tpu as pltpu
from jax.sharding import Mesh
from jax.sharding import PartitionSpec as P

HEAD_DIM = 128
LOCAL_HEADS = 3
COLS = LOCAL_HEADS * HEAD_DIM
PER_SRC = 4
MEMBERS = 8
ROWS = 16
CLEAN = 8
LIST = 16
STRETCHES = 4
KEYS = 256
QUERIES = 256
MASKED = -1e30
UNUSED = 1e30
SCALE = 1.4426950408889634 / math.sqrt(HEAD_DIM)
AXES = ("zh", "xh", "xl", "yh", "yl", "zl", "core")
WIDE = 2 * HEAD_DIM
GROUP = [(0, 1), (1, 0), (3, 0), (2, 1), (1, 1), (3, 1), (2, 0)]
PLANE = [(dx, dy) for dx in (2, 1, 3, 0) for dy in (2, 1, 3, 0) if (dx, dy) != (0, 0)]


class Place:
    def __init__(self):
        for name in AXES:
            setattr(self, name, lax.axis_index(name))
        self.x, self.y, self.z = self.xh * 2 + self.xl, self.yh * 2 + self.yl, self.zh * 2 + self.zl
        self.members = (self.x * 2 + self.yl, self.x * 2 + self.yl, self.y * 2 + self.xl)

    def peer(self, h, d, dl):
        if h < 2:
            px, pyl = (self.x + d) % 4, (self.yl + dl) % 2
            return {"xh": px // 2, "xl": px % 2, "yl": pyl}, px * 2 + pyl
        py, pxl = (self.y + d) % 4, (self.xl + dl) % 2
        return {"yh": py // 2, "yl": py % 2, "xl": pxl}, py * 2 + pxl

    def in_plane(self, dx, dy):
        px, py = (self.x + dx) % 4, (self.y + dy) % 4
        target = {"xh": px // 2, "xl": px % 2, "yh": py // 2, "yl": py % 2}
        return target, px * 2 + py % 2, py * 2 + px % 2

    def half(self, h):
        return jnp.where(h == 2, self.xh, self.yh)

    def to_partner(self, h):
        return {"xh": jnp.where(h == 2, 1 - self.xh, self.xh), "yh": jnp.where(h == 2, self.yh, 1 - self.yh)}

    def position(self, h, index, core):
        if h < 2:
            space = ((index // 32) % 4) * 256 + self.yh * 128 + ((index // 16) % 2) * 64
        else:
            space = self.xh * 512 + ((index // 16) % 2) * 256 + ((index // 32) % 4) * 64
        return space + self.zl * 32 + core * 16 + index % 16

    def to_z(self, step):
        other = (self.z + step + 8) % 8
        return {"zh": other // 2, "zl": other % 2}

    def to_core(self):
        return {"core": 1 - self.core}


def greet(targets):
    barrier = pltpu.get_barrier_semaphore()
    for target in targets:
        pl.semaphore_signal(barrier, inc=1, device_id=target, device_id_type=pl.DeviceIdType.MESH)
    pl.semaphore_wait(barrier, len(targets))


def remote(src, dst, send, recv, target):
    return pltpu.make_async_remote_copy(
        src_ref=src, dst_ref=dst, send_sem=send, recv_sem=recv, device_id=target, device_id_type=pl.DeviceIdType.MESH
    )


def drain(ref, sem):
    pltpu.make_async_copy(ref, ref, sem).wait()


def head_columns(h, member):
    return aligned(member * WIDE + h * HEAD_DIM if h < 2 else MEMBERS * WIDE + member * HEAD_DIM, HEAD_DIM)


def aligned(start, size):
    return pl.ds(pl.multiple_of(start, size), size)


def dot_rows(a, b):
    return lax.dot_general(a, b, (((1,), (1,)), ((), ())), preferred_element_type=jnp.float32)


def merge(parts):
    top = functools.reduce(jnp.maximum, [t for _, t, _ in parts])
    factors = [jnp.exp2(t - top) for _, t, _ in parts]
    total = functools.reduce(jnp.add, [f * n for f, (_, _, n) in zip(factors, parts)])
    sums = functools.reduce(jnp.add, [s.astype(jnp.float32) * f for f, (s, _, _) in zip(factors, parts)])
    return sums, top, total


def read_stats(ref):
    tile = ref[...]
    return [(tile[i : i + 1], tile[2 + i : 3 + i]) for i in (0, 1)]


def write_stats(ref, half, top, total):
    ref[half : half + 1, :] = top
    ref[2 + half : 3 + half, :] = total


def kernel(
    block_list_hbm, list_len_hbm, tok_count_hbm, noise_levels_hbm, q, sk, sv, ck, cv, gate_table, out,
    block_list, list_len, tok_count, noise_levels, scalar_sem, keys0, keys1, keys2, values0, values1, values2, kept, turned, scores0, scores1, staged, stage_sem, queries, own_bias, picked,
    sums, stats, y_got, y_got_stats, joined, joined_stats, z_got, z_got_stats, gates, ready,
    kv_send, kv_recv, core_send, core_recv, q_send, q_recv, ring_send, ring_recv,
    y_send, y_recv, z_send, z_recv, out_send, out_recv, gate_sem,
):
    at = Place()
    keys, values = (keys0, keys1, keys2), (values0, values1, values2)
    staging = [
        pltpu.make_async_copy(ck, staged.at[0, pl.ds(0, CLEAN)], stage_sem.at[0]),
        pltpu.make_async_copy(cv, staged.at[1, pl.ds(0, CLEAN)], stage_sem.at[1]),
        pltpu.make_async_copy(sk, staged.at[0, pl.ds(CLEAN, 1)], stage_sem.at[2]),
        pltpu.make_async_copy(sv, staged.at[1, pl.ds(CLEAN, 1)], stage_sem.at[3]),
    ]
    scalars = [
        pltpu.make_async_copy(src, dst, scalar_sem.at[n])
        for n, (src, dst) in enumerate(
            (
                (block_list_hbm, block_list), (list_len_hbm, list_len), (tok_count_hbm, tok_count),
                (noise_levels_hbm, noise_levels),
            )
        )
    ]
    for copy in staging + scalars:
        copy.start()
    greet([at.in_plane(*off)[0] for off in PLANE] + [*[at.to_z(k) for k in (1, -1, 2, -2)], at.to_core()])

    q_dst = [
        queries.at[at.z, aligned(at.yh * 128 + at.members[0] * ROWS, ROWS), pl.ds(0, WIDE)],
        queries.at[at.z, aligned(at.xh * 128 + at.members[2] * ROWS, ROWS), pl.ds(WIDE, HEAD_DIM)],
    ]

    def q_src(member, other):
        return [q.at[0, :, aligned(member * WIDE, WIDE)], q.at[0, :, head_columns(2, other)]]

    for off in PLANE:
        target, member, other = at.in_plane(*off)
        for src, dst in zip(q_src(member, other), q_dst):
            remote(src, dst, q_send, q_recv, target).start()
    for src, dst in zip(q_src(at.members[0], at.members[2]), q_dst):
        pltpu.make_async_copy(src, dst, q_recv).start()

    my_half = aligned(at.core * 128, 128)

    def send_keys(h):
        for part, ref in enumerate((keys[h], values[h])):
            dst = ref.at[:, aligned((at.core * MEMBERS + at.members[h]) * ROWS, ROWS), :]
            for off in GROUP:
                target, member = at.peer(h, *off)
                cols = head_columns(h, member)
                remote(staged.at[part, :, :, cols], dst, kv_send.at[h, part], kv_recv.at[h, part], target).start()
            cols = head_columns(h, at.members[h])
            pltpu.make_async_copy(staged.at[part, :, :, cols], dst, kv_recv.at[h, part]).start()

    def share_copy(h, part):
        ref = (keys[h], values[h])[part].at[:, my_half, :]
        return remote(ref, ref, core_send.at[h, part], core_recv.at[h, part], at.to_core())

    def share_keys(h):
        for part, ref in enumerate((keys[h], values[h])):
            drain(ref.at[:, my_half, :], kv_recv.at[h, part])
            share_copy(h, part).start()

    def take_keys(h):
        for part in (0, 1):
            share_copy(h, part).wait_recv()

        def turn(block, carry):
            kept[h, block] = keys[h][block]
            turned[h, block] = values[h][block].T
            return carry

        lax.fori_loop(0, CLEAN + 1, turn, 0)

    def ring_copy(h, step, side):
        plane = (at.z - step + 8) % 8 if side == 0 else (at.z + step) % 8
        rows = pl.ds(side * 128, 128) if step == 3 else pl.ds(0, QUERIES)
        piece = queries.at[plane, rows, pl.ds(h * HEAD_DIM, HEAD_DIM)]
        return remote(
            piece, piece, ring_send.at[h, step, side], ring_recv.at[h, step, side], at.to_z(1 if side == 0 else -1)
        )

    def ring_step(h, step):
        for side in (0, 1):
            if step > 0:
                ring_copy(h, step - 1, side).wait_recv()
            ring_copy(h, step, side).start()

    def ring_end(h):
        for side in (0, 1):
            ring_copy(h, 3, side).wait_recv()

    def y_copies(h, dest):
        target = at.to_partner(h)
        src = sums.at[h, dest, :, aligned((1 - at.half(h)) * 128, 128)]
        return [
            remote(src, y_got.at[h, dest], y_send.at[h, dest, 0], y_recv.at[h, dest, 0], target),
            remote(stats.at[h, dest], y_got_stats.at[h, dest], y_send.at[h, dest, 1], y_recv.at[h, dest, 1], target),
        ]

    def send_y(h, dest):
        for copy in y_copies(h, dest):
            copy.start()

    def z_copies(h, dest, slot, step):
        src, target = joined.at[h, dest], at.to_z(step)
        return [
            remote(src, z_got.at[h, slot], z_send.at[h, slot, 0], z_recv.at[h, slot, 0], target),
            remote(
                joined_stats.at[h, dest], z_got_stats.at[h, slot], z_send.at[h, slot, 1], z_recv.at[h, slot, 1], target
            ),
        ]

    def z_start(h, dest, slot, step):
        for copy in z_copies(h, dest, slot, step):
            copy.start()

    def z_part(h, slot):
        drain(z_got.at[h, slot], z_recv.at[h, slot, 0])
        drain(z_got_stats.at[h, slot], z_recv.at[h, slot, 1])
        return (z_got[h, slot], *read_stats(z_got_stats.at[h, slot])[0])

    def own_part(h, dest):
        return (joined[h, dest], *read_stats(joined_stats.at[h, dest])[0])

    def put_joined(h, dest, merged, top, total):
        joined[h, dest] = merged.astype(jnp.bfloat16)
        write_stats(joined_stats.at[h, dest], 0, top, total)

    def middle(h):
        for side in (0, 1):
            dest = (at.z + (6, 2)[side]) % 8

            @pl.when(at.z % 2 == side)
            def _():
                put_joined(h, dest, *merge([own_part(h, dest), z_part(h, 2 + side), z_part(h, 4 + side)]))

            @pl.when(at.z % 2 != side)
            def _():
                put_joined(h, dest, *merge([own_part(h, dest), z_part(h, 2 + side)]))

            z_start(h, dest, 6 + side, (-2, 2)[side])

    def pick_half(h, ref):
        tile = ref[...]
        return [jnp.where(at.half(h) == 0, tile[i : i + 1], tile[i + 1 : i + 2]) for i in (0, 2)]

    def join_y(h, dest):
        for copy in y_copies(h, dest):
            copy.wait_recv()
        merged, top, total = merge(
            [
                (sums[h, dest, :, aligned(at.half(h) * 128, 128)], *pick_half(h, stats.at[h, dest])),
                (y_got[h, dest], *pick_half(h, y_got_stats.at[h, dest])),
            ]
        )
        put_joined(h, dest, merged, top, total)
        away = (at.z - dest + 8) % 8
        above = away < 4

        @pl.when(away % 2 == 1)
        def _():
            slot = jnp.where(above, 0, 1) + jnp.where(jnp.logical_or(away == 3, away == 5), 2, 0)
            z_start(h, dest, slot, jnp.where(above, -1, 1))

        @pl.when(away == 4)
        def _():
            even = at.z % 2 == 0
            z_start(h, dest, jnp.where(even, 4, 5), jnp.where(even, -2, 2))

    stretch_out = (at.zh + 3) % 4

    def finish(h):
        parts = [own_part(h, at.z)] + [z_part(h, slot) for slot in (0, 1, 6, 7)]
        r = lax.broadcasted_iota(jnp.int32, (128, HEAD_DIM), 0)
        position = at.position(h, r, at.core)
        keep = position < tok_count[stretch_out]
        cols = pl.ds(h * HEAD_DIM, HEAD_DIM)
        gate_row = gates[pl.ds(noise_levels[stretch_out], 1), :][:, h * HEAD_DIM : (h + 1) * HEAD_DIM]
        merged, top, total = merge(parts)
        attended = merged / total
        mean_sq = jnp.mean(attended * attended, axis=0, keepdims=True)
        normed = (attended * lax.rsqrt(mean_sq + 1e-6)).T
        ready[:, cols] = jnp.where(keep, normed * gate_row, 0.0).astype(jnp.bfloat16)

        dst = out.at[0, :, head_columns(h, at.members[h])]
        for off in GROUP:
            target, member = at.peer(h, *off)
            remote(ready.at[aligned(member * ROWS, ROWS), cols], dst, out_send.at[h], out_recv.at[h], target).start()
        pltpu.make_async_copy(ready.at[aligned(at.members[h] * ROWS, ROWS), cols], dst, out_recv.at[h]).start()

    def query_rows(h, dest):
        plane = (dest + 6) % 8
        return plane // 2, queries[plane, :, aligned(h * HEAD_DIM, HEAD_DIM)]

    def fold(x, op):
        return op(x.reshape(-1, 8, QUERIES), axis=0)

    def stage(cur, cur_scores, top, nxt, nxt_scores):
        if cur is not None:
            h, dest = cur
            stretch = (dest + 6) % 8 // 2
            shift = top * SCALE
            total8 = jnp.zeros((8, QUERIES), jnp.float32)
            product = None
        if nxt is not None:
            next_h = nxt[0]
            next_stretch, q_head = query_rows(*nxt)
            top8 = jnp.full((8, QUERIES), MASKED, jnp.float32)
        for e in range(PER_SRC):
            rows = slice(e * KEYS, (e + 1) * KEYS)
            if nxt is not None:
                scores = dot_rows(kept[next_h, picked[next_stretch, e]], q_head)
                nxt_scores[rows, :] = scores
                live = e < picked[next_stretch, PER_SRC]
                top8 = jnp.maximum(top8, jnp.where(live, fold(scores, jnp.max), MASKED))
            if cur is not None:
                live = e < picked[stretch, PER_SRC]
                weights = jnp.exp2(cur_scores[rows, :] * SCALE - jnp.where(live, shift, UNUSED))
                total8 = total8 + fold(weights, jnp.sum)
                part = jnp.dot(
                    turned[h, picked[stretch, e]], weights.astype(jnp.bfloat16), preferred_element_type=jnp.float32
                )
                product = part if product is None else product + part
        if cur is not None:
            sums[h, dest] = product.astype(jnp.bfloat16)
            total = jnp.sum(total8, axis=0, keepdims=True)
            for half in (0, 1):
                lanes = slice(half * 128, half * 128 + 128)
                write_stats(stats.at[h, dest], half, shift[:, lanes], total[:, lanes])
        return None if nxt is None else jnp.max(top8, axis=0, keepdims=True)

    def add_own(h, dest):
        @pl.when((dest + 6) % 8 // 2 == at.zh)
        def _():
            _, q_head = query_rows(h, dest)
            bias = own_bias[jnp.where(h == 2, 1, 0)]
            scores = dot_rows(kept[h, CLEAN], q_head) + jnp.concatenate([bias, bias], axis=1)
            top = jnp.max(scores, axis=0, keepdims=True)
            shift = top * SCALE
            weights = jnp.exp2(scores * SCALE - jnp.where(top > 0.5 * MASKED, shift, UNUSED))
            total = jnp.sum(weights, axis=0, keepdims=True)
            product = jnp.dot(turned[h, CLEAN], weights.astype(jnp.bfloat16), preferred_element_type=jnp.float32)
            before = read_stats(stats.at[h, dest])
            for half in (0, 1):
                lanes = slice(half * 128, half * 128 + 128)
                merged, top, total_both = merge(
                    [(sums[h, dest, :, lanes], *before[half]), (product[:, lanes], shift[:, lanes], total[:, lanes])]
                )
                sums[h, dest, :, lanes] = merged.astype(jnp.bfloat16)
                write_stats(stats.at[h, dest], half, top, total_both)

    gate_copies = [
        pltpu.make_async_copy(
            gate_table.at[:, aligned(at.members[0] * WIDE, WIDE)], gates.at[:, pl.ds(0, WIDE)], gate_sem.at[0]
        ),
        pltpu.make_async_copy(
            gate_table.at[:, head_columns(2, at.members[2])], gates.at[:, pl.ds(WIDE, HEAD_DIM)], gate_sem.at[1]
        ),
    ]

    for copy in staging:
        copy.wait()
    for h in range(LOCAL_HEADS):
        send_keys(h)
    for copy in gate_copies:
        copy.start()
    for copy in scalars:
        copy.wait()
    for stretch in range(STRETCHES):
        count = jnp.int32(0)
        chosen = [jnp.int32(0)] * PER_SRC
        for entry in range(LIST):
            block = block_list[stretch, entry]
            hit = jnp.logical_and(block // CLEAN == at.zh, entry < list_len[stretch])
            for e in range(PER_SRC):
                chosen[e] = jnp.where(jnp.logical_and(hit, count == e), block % CLEAN, chosen[e])
            count = count + jnp.where(hit, 1, 0)
        for e in range(PER_SRC):
            picked[stretch, e] = chosen[e]
        picked[stretch, PER_SRC] = count
    j = lax.broadcasted_iota(jnp.int32, (KEYS, 128), 0)
    for n, h in enumerate((0, 2)):
        own_bias[n] = jnp.where(at.position(h, j % 128, j // 128) < tok_count[at.zh], 0.0, MASKED)
    drain(queries.at[at.z], q_recv)
    for step in (0, 1):
        for h in (0, 1):
            ring_step(h, step)
    ring_step(2, 0)
    share_keys(0)
    for copy in gate_copies:
        copy.wait()
    take_keys(0)

    def unit_at(p):
        near, far = p < 10, p < 16
        h = jnp.where(near, p // 5, jnp.where(far, p % 2, 2))
        u = jnp.where(near, p % 5, jnp.where(far, p // 2, p - 16))
        near_first = 2 + jnp.where(u % 2 == 1, (u + 1) // 2, 8 - u // 2)
        far_first = jnp.where(u % 2 == 1, 3 - u // 2, 4 + u // 2)
        return h, (at.z + jnp.where(far, near_first, far_first)) % 8

    def pair(i, top):
        for h in (0, 1):
            pl.when(i == 1)(functools.partial(ring_step, h, 2))
        pl.when(i == 2)(lambda: ring_step(2, 1))
        pl.when(i == 2)(lambda: share_keys(1))
        pl.when(i == 2)(lambda: take_keys(1))
        for h in (0, 1):
            pl.when(i == 3)(functools.partial(ring_step, h, 3))
        pl.when(i == 4)(lambda: ring_step(2, 2))
        for h in (0, 1):
            pl.when(i == 6)(functools.partial(ring_end, h))
        pl.when(i == 6)(lambda: ring_step(2, 3))
        pl.when(i == 6)(lambda: share_keys(2))
        pl.when(i == 7)(lambda: take_keys(2))
        pl.when(i == 9)(lambda: ring_end(2))
        even, odd, later = unit_at(2 * i), unit_at(2 * i + 1), unit_at(jnp.minimum(2 * i + 2, 23))
        top = stage(even, scores0, top, odd, scores1)
        add_own(*even)
        send_y(*even)
        top = stage(odd, scores1, top, later, scores0)
        add_own(*odd)
        send_y(*odd)

        @pl.when(i >= 6)
        def _():
            lax.fori_loop(3 * i - 18, 3 * i - 15, join_far, 0)

        pl.when(i == 11)(lambda: middle(0))

        return top

    def is_near(dest):
        return (at.z - dest + 9) % 8 < 3

    def join_far(p, carry):
        h, dest = unit_at(p)
        pl.when(jnp.logical_not(is_near(dest)))(lambda: join_y(h, dest))
        return carry

    def join_near(p, carry):
        h, dest = unit_at(p)
        pl.when(is_near(dest))(lambda: join_y(h, dest))
        return carry

    def join(p, carry):
        join_y(*unit_at(p))
        return carry

    lax.fori_loop(0, 12, pair, stage(None, None, None, unit_at(0), scores0))
    middle(1)
    lax.fori_loop(18, 21, join, 0)
    middle(2)
    lax.fori_loop(0, 18, join_near, 0)
    finish(0)
    lax.fori_loop(21, 24, join, 0)
    finish(1)
    finish(2)

    drain(queries.at[0, pl.ds(0, 15 * ROWS), :], q_send)
    for h in range(LOCAL_HEADS):
        for part, ref in enumerate((keys[h], values[h])):
            drain(ref.at[:, pl.ds(0, 7 * ROWS), :], kv_send.at[h, part])
            share_copy(h, part).wait_send()
        for side in (0, 1):
            for step in range(4):
                ring_copy(h, step, side).wait_send()
        for k in range(8):
            for copy in y_copies(h, (at.z + k) % 8):
                copy.wait_send()
        for slot in (0, 1, 2, 3, 6, 7):
            for copy in z_copies(h, at.z, slot, 1):
                copy.wait_send()
        for copy in z_copies(h, at.z, 4 + at.z % 2, 1):
            copy.wait_send()
        drain(ready.at[pl.ds(0, 7 * ROWS), pl.ds(0, HEAD_DIM)], out_send.at[h])
        drain(out.at[0, :, pl.ds(0, MEMBERS * HEAD_DIM)], out_recv.at[h])


def shards(q, sk, sv, ck, cv, block_list, list_len, tok_count, noise_levels, gate_table):
    hbm = pl.BlockSpec(memory_space=pltpu.HBM)
    dma = pltpu.SemaphoreType.DMA
    bf, f32 = jnp.bfloat16, jnp.float32
    heads = LOCAL_HEADS
    return pl.pallas_call(
        kernel,
        out_shape=jax.ShapeDtypeStruct((1, ROWS, MEMBERS * COLS), bf),
        in_specs=[hbm] * 10,
        out_specs=hbm,
        scratch_shapes=[
            pltpu.SMEM((STRETCHES, LIST), jnp.int32),
            *[pltpu.SMEM((STRETCHES,), jnp.int32)] * 3,
            dma((4,)),
        ]
        + [pltpu.VMEM((CLEAN + 1, KEYS, HEAD_DIM), bf)] * 6
        + [
            pltpu.VMEM((heads, CLEAN + 1, KEYS, HEAD_DIM), bf),
            pltpu.VMEM((heads, CLEAN + 1, HEAD_DIM, KEYS), bf),
            pltpu.VMEM((PER_SRC * KEYS, QUERIES), f32),
            pltpu.VMEM((PER_SRC * KEYS, QUERIES), f32),
            pltpu.VMEM((2, CLEAN + 1, ROWS, MEMBERS * COLS), bf),
            dma((4,)),
            pltpu.VMEM((8, QUERIES, COLS), bf),
            pltpu.VMEM((2, KEYS, 128), f32),
            pltpu.SMEM((STRETCHES, PER_SRC + 1), jnp.int32),
            pltpu.VMEM((heads, 8, HEAD_DIM, QUERIES), bf),
            pltpu.VMEM((heads, 8, 8, 128), f32),
            pltpu.VMEM((heads, 8, HEAD_DIM, 128), bf),
            pltpu.VMEM((heads, 8, 8, 128), f32),
            pltpu.VMEM((heads, 8, HEAD_DIM, 128), bf),
            pltpu.VMEM((heads, 8, 8, 128), f32),
            pltpu.VMEM((heads, 8, HEAD_DIM, 128), bf),
            pltpu.VMEM((heads, 8, 8, 128), f32),
            pltpu.VMEM((48, COLS), f32),
            pltpu.VMEM((128, COLS), bf),
            dma((heads, 2)), dma((heads, 2)), dma((heads, 2)), dma((heads, 2)), dma, dma,
            dma((heads, 4, 2)), dma((heads, 4, 2)), dma((heads, 8, 2)), dma((heads, 8, 2)),
            dma((heads, 8, 2)), dma((heads, 8, 2)), dma((heads,)), dma((heads,)), dma((2,)),
        ],
        compiler_params=pltpu.CompilerParams(
            collective_id=0, has_side_effects=True, vmem_limit_bytes=58 * 1024 * 1024
        ),
    )(block_list, list_len, tok_count, noise_levels, q, sk, sv, ck, cv, gate_table)


def solution(mesh):
    fine = Mesh(mesh.devices.reshape(4, 2, 2, 2, 2, 2, 2), AXES)
    split = P("zh", ("xh", "xl", "yh", "yl", "zl", "core"), None)
    return jax.shard_map(
        shards, mesh=fine, in_specs=(split,) * 5 + (P(),) * 5, out_specs=split, check_vma=False
    )
```
